256 devices in a mesh: section: 8 (over y, core), expert: 32 (over z, x).
Axes of the slice: x: 4, y: 4, z: 8, core: 2. Of those that a mesh axis runs over, the one named last changes fastest.
Arguments:
- tokens_ahead: bfloat16 [8, 512, 3584], P('section', 'expert'), may hold values from -6 to 6
- tokens_behind: bfloat16 [8, 512, 3584], P('section', 'expert'), may hold values from -6 to 6
- routes_ahead: int32 [1, 8, 512, 8], P(None, None, 'expert'), may hold values from 0 to 31, all different within a row; in each aligned block of 16 rows (0 to 15, 16 to 31, ..., all dimensions but the last counted through in order) at most 5 rows name the same one
- routes_behind: int32 [1, 8, 512, 8], P(None, None, 'expert'), may hold values from 0 to 31, all different within a row; in each aligned block of 16 rows (0 to 15, 16 to 31, ..., all dimensions but the last counted through in order) at most 5 rows name the same one
- gates_ahead: float32 [1, 8, 512, 8], P(None, None, 'expert'), may hold values from 0.1 to 1
- gates_behind: float32 [1, 8, 512, 8], P(None, None, 'expert'), may hold values from 0.1 to 1
- gate_proj: bfloat16 [8, 32, 3584, 512], P('section', 'expert'), may hold values from -0.09375 to 0.09375
- up_proj: bfloat16 [8, 32, 3584, 512], P('section', 'expert'), may hold values from -0.09375 to 0.09375
- down_proj: bfloat16 [8, 32, 512, 3584], P('section', 'expert'), may hold values from -0.1875 to 0.1875
Outputs:
- ahead_states: bfloat16 [8, 512, 3584], P('section', 'expert')
- behind_states: bfloat16 [8, 512, 3584], P('section', 'expert')
The draws below stay inside these ranges and needn't reach their ends.
Inputs may be any that keep to these rules, and one draw needn't show every extreme that they name: `routes_ahead`: in each aligned block of 16 tokens (the tokens of one device) no expert is named by more than 5 routes, a bound that some block reaches; a token names 8 different experts. `routes_behind`: in each aligned block of 16 tokens no expert is named by more than 5 routes, a bound that some block reaches; a token names 8 different experts.
All inputs are finite; a program needn't handle non-finite values.
Results may differ from the reference program's by a relative error of at most 0.01.
Values may be sent and summed in bfloat16 or wider, within the bound.
A program may use at most 128 MiB of HBM per device.

```python
import math
import jax
import jax.numpy as jnp
import numpy as np
from jax import lax

D = 3584
FF = 1024
TOP = 8
STEPS = 1
TOK_DEV = 16
HALF_FF = 512
LAYERS = 4
EXPERTS = 32
HALF_TOKENS = 512
CAP = 5
N_SECTION = 8


def block_levels(rng, shape, shards, least, high):
    loudness, own = 1.0, jax.random.fold_in(rng, 6)
    for dim, shards_of in shards:
        heights = jnp.exp(jax.random.uniform(jax.random.fold_in(own, dim), (shards_of,), jnp.float32, least / len(shards), high / len(shards)))
        loudness = loudness * jnp.repeat(heights, shape[dim] // shards_of).reshape([-1 if axis == dim else 1 for axis in range(len(shape))])
    return loudness


def shared_out(own_key, own, number, rows, amount, top, bound, skew):
    ranking = jax.random.permutation(own_key, amount)
    packed, common = load_shares(amount, rows * top, bound, skew, True), load_shares(amount, rows * top, bound, skew, False)
    places = jnp.arange(amount)

    def named(lengths, rotation):
        used = int((lengths > 0).sum())
        fixed = max(1, used // 4)
        passed = fixed + (places - fixed + rotation * (used - fixed)) % max(1, amount - fixed)
        return jnp.zeros((amount,), jnp.int32).at[ranking[jnp.where(places < fixed, places, passed)]].set(jnp.asarray(lengths, jnp.int32))

    lengths = jnp.where(number % 4 == 0, named(packed, number // 4), named(common, number - number // 4 - 1))
    mixed = jax.random.permutation(jax.random.fold_in(own, 3), amount)
    donor, taker = mixed[0:amount // 2 * 2:2], mixed[1:amount // 2 * 2:2]
    slack = jnp.minimum(lengths[donor] - 1, bound - lengths[taker]) // 2
    slack = jnp.where((donor == ranking[0]) | (taker == ranking[0]) | (lengths[taker] == 0), 0, jnp.maximum(slack, 0))
    passed = jax.random.randint(jax.random.fold_in(own, 4), (amount // 2,), 0, 1 << 20) % (slack + 1)
    lengths = lengths.at[donor].add(-passed).at[taker].add(passed)
    members = jnp.searchsorted(jnp.cumsum(lengths), jnp.arange(rows * top), side="right").astype(jnp.int32)
    grid = members.reshape(top, rows).T
    grid = grid[jax.random.permutation(jax.random.fold_in(own, 1), rows)]
    rotation = jax.random.randint(jax.random.fold_in(own, 2), (rows, 1), 0, top)
    return jnp.take_along_axis(grid, (jnp.arange(top)[None, :] + rotation) % top, axis=1)


def load_shares(amount, total, bound, lean, full):
    weights = [(1 << 20) // math.isqrt(standing ** lean) + 1 for standing in range(1, amount + 1)]
    largest = bound if full else min(bound, max(-(-total // amount), total * weights[0] // sum(weights)))
    least = 1 if total - largest >= amount - 1 else 0
    holding, rest = [largest] + [least] * (amount - 1), total - largest - least * (amount - 1)
    while rest > 0:
        free = [i for i in range(1, amount) if holding[i] < largest] or [i for i in range(1, amount) if holding[i] < bound]
        whole, remaining = sum([weights[i] for i in free]), rest
        for i in free:
            addition = min(bound - holding[i], max(1, remaining * weights[i] // whole), rest)
            holding[i] = holding[i] + addition
            rest = rest - addition
    return np.array(holding)


def noise(stream_key, extent, spread, most, pieces=(), kind=jnp.bfloat16):
    values = spread * jax.random.normal(stream_key, extent, jnp.float32)
    if pieces:
        values = values * block_levels(stream_key, extent, pieces, -0.22, 0.18)
    return jnp.clip(values, -most, most).astype(kind)


def setup_inputs(seed: int = 0) -> dict:
    streams_of = jax.random.split(jax.random.key(seed), 10)
    tokens_ahead = noise(streams_of[0], (N_SECTION, HALF_TOKENS, D), 1.0, 6.0, ((0, 8), (1, 32)))
    tokens_behind = noise(streams_of[1], (N_SECTION, HALF_TOKENS, D), 1.0, 6.0, ((0, 8), (1, 32)))
    routes_ahead_keys = jax.random.split(jax.random.fold_in(streams_of[2], 1), STEPS * N_SECTION * HALF_TOKENS // TOK_DEV)
    routes_ahead_turns = jax.random.permutation(jax.random.fold_in(streams_of[2], 3), STEPS * N_SECTION * HALF_TOKENS // TOK_DEV)
    routes_ahead = jax.vmap(lambda own, number: shared_out(jax.random.fold_in(streams_of[2], 2), own, number, TOK_DEV, EXPERTS, TOP, CAP, 2))(routes_ahead_keys, routes_ahead_turns).reshape((STEPS, N_SECTION, HALF_TOKENS, TOP))
    routes_behind_keys = jax.random.split(jax.random.fold_in(streams_of[3], 1), STEPS * N_SECTION * HALF_TOKENS // TOK_DEV)
    routes_behind_turns = jax.random.permutation(jax.random.fold_in(streams_of[3], 3), STEPS * N_SECTION * HALF_TOKENS // TOK_DEV)
    routes_behind = jax.vmap(lambda own, number: shared_out(jax.random.fold_in(streams_of[3], 2), own, number, TOK_DEV, EXPERTS, TOP, CAP, 2))(routes_behind_keys, routes_behind_turns).reshape((STEPS, N_SECTION, HALF_TOKENS, TOP))
    gates_ahead = jnp.clip(jnp.exp(math.log(1.0) - 2.3025851 * jax.random.uniform(streams_of[4], (STEPS, N_SECTION, HALF_TOKENS, TOP), jnp.float32) ** block_levels(streams_of[4], (STEPS, N_SECTION, HALF_TOKENS, TOP), ((2, 32),), -0.2, 0.2)), 0.1, 1.0)
    gates_behind = jnp.clip(jnp.exp(math.log(1.0) - 2.3025851 * jax.random.uniform(streams_of[5], (STEPS, N_SECTION, HALF_TOKENS, TOP), jnp.float32) ** block_levels(streams_of[5], (STEPS, N_SECTION, HALF_TOKENS, TOP), ((2, 32),), -0.2, 0.2)), 0.1, 1.0)
    gate_proj = noise(streams_of[6], (N_SECTION, EXPERTS, D, HALF_FF), D ** -0.5, 0.09375, ((0, 8), (1, 32)))
    up_proj = noise(streams_of[7], (N_SECTION, EXPERTS, D, HALF_FF), D ** -0.5, 0.09375, ((0, 8), (1, 32)))
    down_proj = noise(streams_of[8], (N_SECTION, EXPERTS, HALF_FF, D), FF ** -0.5, 0.1875, ((0, 8), (1, 32)))
    return {"tokens_ahead": tokens_ahead, "tokens_behind": tokens_behind, "routes_ahead": routes_ahead, "routes_behind": routes_behind, "gates_ahead": gates_ahead, "gates_behind": gates_behind, "gate_proj": gate_proj, "up_proj": up_proj, "down_proj": down_proj}


def normalize(buffer):
    values = buffer.astype(jnp.float32)
    scale_row = lax.rsqrt(lax.optimization_barrier(jnp.mean(values * values, axis=-1, keepdims=True)) + 1e-06)
    return (values * scale_row).astype(jnp.bfloat16)

def slot_index(ids, experts_n, capacity):
    flat_ids = ids.reshape(-1).astype(jnp.int32)
    onehot = (flat_ids[:, None] == jnp.arange(experts_n, dtype=jnp.int32)[None, :]).astype(jnp.int32)
    before = (jnp.cumsum(onehot, axis=0) - onehot).astype(jnp.int32)
    position = lax.optimization_barrier(jnp.sum(before * onehot, axis=1)).astype(jnp.int32)
    return (flat_ids * capacity + position).astype(jnp.int32)

def dispatch_matrix(slot_ids, row_count, top_count, slot_total):
    matches = slot_ids.reshape(row_count, top_count)[None, :, :] == jnp.arange(slot_total, dtype=jnp.int32)[:, None, None]
    return jnp.any(matches, axis=2).astype(jnp.bfloat16)

def expert(arrived, gate_local, up_local, down_local):
    gate_out = jnp.dot(arrived, gate_local, preferred_element_type=jnp.float32)
    up_out = jnp.dot(arrived, up_local, preferred_element_type=jnp.float32)
    hidden = (jax.nn.silu(gate_out) * up_out).astype(jnp.bfloat16)
    return jnp.dot(hidden, down_local, preferred_element_type=jnp.float32).astype(jnp.bfloat16)

def mixing(slot_ids, gate_weights, returned):
    row_count, top_count = gate_weights.shape
    picked = jnp.take(returned, slot_ids, axis=0).reshape(row_count, top_count, -1).astype(jnp.float32)
    return jnp.einsum('rk,rkd->rd', gate_weights.astype(jnp.float32), picked)

def layer_pair(states, ids, gate_weights, gate_half, up_half, down_half):
    blocks = HALF_TOKENS // TOK_DEV
    slot_total = EXPERTS * CAP
    normed = normalize(states).reshape(2, blocks, TOK_DEV, D)
    slot_ids = jax.vmap(jax.vmap(lambda part_ids: slot_index(part_ids, EXPERTS, CAP)))(ids.reshape(2, blocks, TOK_DEV, TOP))

    def build(slot_part, normed_part):
        matrix = dispatch_matrix(slot_part, TOK_DEV, TOP, slot_total)
        return jnp.dot(matrix, normed_part, preferred_element_type=jnp.float32).astype(jnp.bfloat16)
    outgoing = jax.vmap(jax.vmap(build))(slot_ids, normed).reshape(2, blocks, EXPERTS, CAP, D)
    arrived = jnp.transpose(outgoing, (2, 0, 1, 3, 4)).reshape(EXPERTS, 2 * blocks * CAP, D)
    weights_split = gate_weights.reshape(2, blocks, TOK_DEV, TOP)
    total = states.astype(jnp.float32)
    for half_index in range(2):
        produced = lax.map(lambda a: expert(a[0], a[1], a[2], a[3]), (arrived, gate_half[half_index], up_half[half_index], down_half[half_index]))
        returned = jnp.transpose(produced.reshape(EXPERTS, 2, blocks, CAP, D), (1, 2, 0, 3, 4)).reshape(2, blocks, slot_total, D)
        mixed = jax.vmap(jax.vmap(mixing))(slot_ids, weights_split, returned)
        total = total + mixed.reshape(2, HALF_TOKENS, D)
    return total.astype(jnp.bfloat16)

def reference(tokens_ahead, tokens_behind, routes_ahead, routes_behind, gates_ahead, gates_behind, gate_proj, up_proj, down_proj):
    gate_pairs = gate_proj.reshape(LAYERS, 2, EXPERTS, D, HALF_FF)
    up_pairs = up_proj.reshape(LAYERS, 2, EXPERTS, D, HALF_FF)
    down_pairs = down_proj.reshape(LAYERS, 2, EXPERTS, HALF_FF, D)

    def all_layers(states, ids, gate_weights):
        paired = (states.reshape(LAYERS, 2, HALF_TOKENS, D), ids.reshape(LAYERS, 2, HALF_TOKENS, TOP), gate_weights.reshape(LAYERS, 2, HALF_TOKENS, TOP), gate_pairs, up_pairs, down_pairs)
        result = lax.map(lambda a: layer_pair(a[0], a[1], a[2], a[3], a[4], a[5]), paired)
        return result.reshape(N_SECTION, HALF_TOKENS, D)
    ahead_state = tokens_ahead
    behind_state = tokens_behind
    for turn_index in range(STEPS):
        ahead_state = jnp.concatenate([ahead_state[-2:], ahead_state[:-2]], axis=0)
        behind_state = jnp.concatenate([behind_state[2:], behind_state[:2]], axis=0)
        ahead_state = all_layers(ahead_state, routes_ahead[turn_index], gates_ahead[turn_index])
        behind_state = all_layers(behind_state, routes_behind[turn_index], gates_behind[turn_index])
    return (ahead_state, behind_state)
```

```python
import jax
import jax.numpy as jnp
from jax import lax
from jax.experimental import pallas as pl
from jax.experimental.pallas import tpu as pltpu
from jax.sharding import PartitionSpec as P

MESH = pl.DeviceIdType.MESH
F32 = jnp.float32
BF16 = jnp.bfloat16

WIDTH = 3584
HALF = 512
ROWS = 16
TOP = 8
CAP = 5
CHUNKS = 2
COLS = WIDTH // CHUNKS
FOLD = COLS // 2
ITEMS = 2 * CHUNKS
NX = 4
NZ = 8
OFFSETS = (0, 1, -1, 2, -2, 3, -3, 4)


def parents(chunk):
    return (None, 0, 0, 1, 2, 3, 4, 5 if chunk % 2 == 0 else 6)


def children(chunk, slot):
    return [i for i in range(NZ) if parents(chunk)[i] == slot]


def tiles(width, step, body):
    @pl.loop(0, width // step)
    def _(j):
        body(pl.multiple_of(j * step, step))


def dot(a, b):
    return jnp.dot(a, b, preferred_element_type=F32)


def kernel(
    tok_a, tok_b, ids_a, ids_b, gates_a, gates_b, gate_hbm, up_hbm, down_hbm,
    out_a, out_b,
    wgu, wdn, state, meta, sel, mixw, xg, snd, sndl, xs, fold, acc, hid, yo, yx, yr,
    ret, retl, rb, rbl, ct, rss, rsr,
    w_sem, y_s, y_r, m_s, m_r, ag_s, ag_r, x_s, x_r, ex_s, ex_r, yx_s, yx_r, rt_s, rt_r, rs_s, rs_r,
):
    section = lax.axis_index("section")
    place = lax.axis_index("expert")
    z_at, x_at = place // NX, place % NX
    partner = (section + 1 - 2 * (section % 2), place)

    def along_y(layers):
        return ((section + 2 * layers + 8) % 8, place)

    def along_z(steps):
        return (section, ((z_at + steps + 2 * NZ) % NZ) * NX + x_at)

    def along_x(steps):
        return (section, z_at * NX + (x_at + steps + NX) % NX)

    tokens = (tok_a, tok_b)
    outs = (out_a, out_b)
    sent = []

    def remote(src, dst, send, recv, device):
        return pltpu.make_async_remote_copy(
            src_ref=src, dst_ref=dst, send_sem=send, recv_sem=recv, device_id=device, device_id_type=MESH
        )

    def start(copy):
        copy.start()
        sent.append(copy)

    def y_copy(s):
        return remote(tokens[s].at[0], state.at[s], y_s.at[s], y_r.at[s], along_y(1 if s == 0 else -1))

    def meta_copy(i):
        return remote(
            meta.at[pl.ds(0, ROWS)], meta.at[pl.ds(ROWS * i, ROWS)], m_s.at[i], m_r.at[i], along_z(OFFSETS[i])
        )

    def ag_copy(q, i):
        p = parents(q % CHUNKS)[i]
        return remote(
            xg.at[q, pl.ds(ROWS * p, ROWS)], xg.at[q, pl.ds(ROWS * i, ROWS)],
            ag_s.at[q, i], ag_r.at[q, i], along_z(OFFSETS[i] - OFFSETS[p]),
        )

    def x_copy(q, u, dx):
        sems = (x_s.at[q, u, dx], x_r.at[q, u, dx], along_x(dx))
        rows = pl.ds(16 * dx, 16)
        if u == 2:
            return remote(sndl.at[q, rows], fold.at[q, 0, rows], *sems)
        return remote(snd.at[q, u, rows], xs.at[q, pl.ds(64 * u + 16 * dx, 16)], *sems)

    def ex_copy(q, u):
        sems = (ex_s.at[q, u], ex_r.at[q, u], partner)
        if u == 2:
            return remote(fold.at[q, 0], fold.at[q, 1], *sems)
        return remote(xs.at[q, pl.ds(64 * u, 64)], xs.at[q, pl.ds(128 + 64 * u, 64)], *sems)

    def yx_copy(q):
        return remote(yx.at[q], yr.at[q], yx_s.at[q], yx_r.at[q], partner)

    def rt_copy(q, u, dx):
        sems = (rt_s.at[q, u, dx], rt_r.at[q, u, dx], along_x(-dx))
        rows = pl.ds(16 * dx, 16)
        if u == 2:
            return remote(retl.at[q, rows], rbl.at[q, rows], *sems)
        return remote(ret.at[q, u, rows], rb.at[q, u, rows], *sems)

    def rs_copy(q, i):
        p = parents(q % CHUNKS)[i]
        rows = pl.ds(ROWS * i, ROWS)
        return remote(
            rss.at[q, rows], rsr.at[q, rows], rs_s.at[q, i], rs_r.at[q, i], along_z(OFFSETS[p] - OFFSETS[i])
        )

    loads = [
        pltpu.make_async_copy(gate_hbm.at[0, 0], wgu.at[:, pl.ds(0, HALF)], w_sem.at[0]),
        pltpu.make_async_copy(up_hbm.at[0, 0], wgu.at[:, pl.ds(HALF, HALF)], w_sem.at[1]),
        pltpu.make_async_copy(down_hbm.at[0, 0], wdn, w_sem.at[2]),
    ]
    for load in loads:
        load.start()

    barrier = pltpu.get_barrier_semaphore()
    friends = [along_y(1), along_y(-1), partner]
    friends += [along_z(OFFSETS[i]) for i in range(1, NZ)]
    friends += [along_x(dx) for dx in range(1, NX)]
    for friend in friends:
        pl.semaphore_signal(barrier, inc=1, device_id=friend, device_id_type=MESH)

    lane8 = lax.broadcasted_iota(jnp.int32, (TOP, 128), 1)
    row8 = lax.broadcasted_iota(jnp.int32, (TOP, 128), 0)
    block = jnp.zeros((ROWS, 128), F32)
    for s, (ids_ref, gates_ref) in enumerate(((ids_a, gates_a), (ids_b, gates_b))):
        ids = ids_ref[0, section].astype(F32).astype(BF16)
        gates = gates_ref[0, section]
        high = gates.astype(BF16)
        low = (gates - high.astype(F32)).astype(BF16)
        for j, part in enumerate((ids, high, low)):
            spot = jnp.where(lane8 == row8 + (24 * s + 8 * j), 1.0, 0.0).astype(BF16)
            block = block + dot(part, spot)
    meta[0:ROWS, :] = block.astype(BF16)

    pl.semaphore_wait(barrier, len(friends))

    def y_start(s):
        start(y_copy(s))

    def norm(s):
        y_copy(s).wait_recv()
        values = state[s].astype(F32)
        scale = lax.rsqrt(jnp.mean(values * values, axis=-1, keepdims=True) + 1e-06)
        normed = (values * scale).astype(BF16)
        for c in range(CHUNKS):
            xg[s * CHUNKS + c, 0:ROWS, :] = normed[:, c * COLS:(c + 1) * COLS]

    def z_send(q, slot):
        for i in children(q % CHUNKS, slot):
            start(ag_copy(q, i))

    def z_forward(q, slot):
        ag_copy(q, slot).wait_recv()
        z_send(q, slot)

    def plan():
        for i in range(1, NZ):
            meta_copy(i).wait_recv()
        table = meta[...].astype(F32).T
        lane = lax.broadcasted_iota(jnp.int32, (128, 128), 1)
        row = lax.broadcasted_iota(jnp.int32, (128, 128), 0)
        earlier = jnp.where((row // ROWS == lane // ROWS) & (row < lane), 1.0, 0.0).astype(BF16)
        first = (lax.broadcasted_iota(jnp.int32, (1, 128), 1) // ROWS) * CAP
        for s in range(2):
            ids_t, high_t, low_t = (table[24 * s + 8 * j:24 * s + 8 * j + 8] for j in range(3))
            named, highs, lows = [], [], []
            for dx in range(NX):
                expert_at = (z_at * NX + (x_at + dx) % NX).astype(F32)
                same = jnp.where(ids_t == expert_at, 1.0, 0.0)
                named.append(jnp.sum(same, axis=0, keepdims=True))
                highs.append(jnp.sum(same * high_t, axis=0, keepdims=True))
                lows.append(jnp.sum(same * low_t, axis=0, keepdims=True))
            stacked = jnp.concatenate(named + [jnp.zeros((8 - NX, 128), F32)], axis=0)
            before = dot(stacked.astype(BF16), earlier)
            for u, (least, most, shift) in enumerate(((0, 16, 0), (16, 32, 0), (32, 48, 0), (32, 48, 8))):
                picks = jnp.zeros((128, 128), F32)
                high_w = jnp.zeros((128, 128), F32)
                low_w = jnp.zeros((128, 128), F32)
                for dx in range(NX):
                    spot = first + before[dx:dx + 1].astype(jnp.int32)
                    here = (named[dx] > 0.5) & (spot >= least) & (spot < most)
                    target = jnp.where(here, spot - least + shift + 16 * dx, -1)
                    hit = row == target
                    picks = picks + jnp.where(hit, 1.0, 0.0)
                    high_w = high_w + jnp.where(hit, highs[dx], 0.0)
                    low_w = low_w + jnp.where(hit, lows[dx], 0.0)
                sel[s, u] = picks[0:64].astype(BF16)
                mixw[s, u, 0] = high_w.T.astype(BF16)
                mixw[s, u, 1] = low_w.T.astype(BF16)

    def select(q, u):
        s = q // CHUNKS
        if u == 2:
            def body(at):
                value = dot(sel[s, 2], xg[q, :, pl.ds(at, 128)])
                value = value + dot(sel[s, 3], xg[q, :, pl.ds(FOLD + at, 128)])
                value = value.astype(BF16)
                fold[q, 0, 0:16, pl.ds(at, 128)] = value[0:16]
                sndl[q, 16:64, pl.ds(at, 128)] = value[16:64]
            tiles(FOLD, 128, body)
        else:
            depth = 64 if u == 0 else 112

            def body(at):
                value = dot(sel[s, u][:, 0:depth], xg[q, 0:depth, pl.ds(at, 256)]).astype(BF16)
                xs[q, 64 * u:64 * u + 16, pl.ds(at, 256)] = value[0:16]
                snd[q, u, 16:64, pl.ds(at, 256)] = value[16:64]
            tiles(COLS, 256, body)
        for dx in (2, 1, 3):
            start(x_copy(q, u, dx))

    def exchange(q, u):
        for dx in (1, 3, 2):
            x_copy(q, u, dx).wait_recv()
        start(ex_copy(q, u))

    def gate_up(q):
        s, c = q // CHUNKS, q % CHUNKS
        for u in range(3):
            ex_copy(q, u).wait_recv()

        def unfold(at):
            for h in range(2):
                part = fold[q, h, :, pl.ds(at, 128)].astype(F32)
                left = jnp.concatenate([part[16 * dx:16 * dx + 8] for dx in range(NX)], axis=0)
                right = jnp.concatenate([part[16 * dx + 8:16 * dx + 16] for dx in range(NX)], axis=0)
                xs[q, 256 + 32 * h:288 + 32 * h, pl.ds(at, 128)] = left.astype(BF16)
                xs[q, 256 + 32 * h:288 + 32 * h, pl.ds(FOLD + at, 128)] = right.astype(BF16)
        tiles(FOLD, 128, unfold)

        def body(at):
            value = dot(xs[q], wgu[c * COLS:(c + 1) * COLS, pl.ds(at, 256)])
            if c == 0:
                acc[:, pl.ds(at, 256)] = value
            else:
                acc[:, pl.ds(at, 256)] = acc[:, pl.ds(at, 256)] + value
        tiles(2 * HALF, 256, body)

    def activate(s):
        def body(at):
            gate = acc[:, pl.ds(at, 128)]
            up = acc[:, pl.ds(HALF + at, 128)]
            hid[s, :, pl.ds(at, 128)] = (gate / (1.0 + jnp.exp(-gate)) * up).astype(BF16)
        tiles(HALF, 128, body)

    def down(q):
        s, c = q // CHUNKS, q % CHUNKS

        def body(at):
            value = dot(hid[s], wdn[:, pl.ds(c * COLS + at, 256)])
            yo[q, 0:128, pl.ds(at, 256)] = value[0:128]
            yo[q, 128:160, pl.ds(at, 256)] = value[256:288]
            yx[q, 0:128, pl.ds(at, 256)] = value[128:256].astype(BF16)
            yx[q, 128:160, pl.ds(at, 256)] = value[288:320].astype(BF16)
        tiles(COLS, 256, body)
        start(yx_copy(q))

    def send_back(q):
        yx_copy(q).wait_recv()

        def left(at):
            near = yo[q, 128:160, pl.ds(at, 128)] + yr[q, 128:160, pl.ds(at, 128)].astype(F32)
            far = yo[q, 128:160, pl.ds(FOLD + at, 128)] + yr[q, 128:160, pl.ds(FOLD + at, 128)].astype(F32)
            for dx in range(NX):
                both = jnp.concatenate([near[8 * dx:8 * dx + 8], far[8 * dx:8 * dx + 8]], axis=0).astype(BF16)
                (rbl if dx == 0 else retl)[q, 16 * dx:16 * dx + 16, pl.ds(at, 128)] = both
        tiles(FOLD, 128, left)
        for dx in (2, 1, 3):
            start(rt_copy(q, 2, dx))
        for u in (1, 0):
            def main(at):
                rows = pl.ds(64 * u, 64)
                both = (yo[q, rows, pl.ds(at, 256)] + yr[q, rows, pl.ds(at, 256)].astype(F32)).astype(BF16)
                rb[q, u, 0:16, pl.ds(at, 256)] = both[0:16]
                ret[q, u, 16:64, pl.ds(at, 256)] = both[16:64]
            tiles(COLS, 256, main)
            for dx in (2, 1, 3):
                start(rt_copy(q, u, dx))

    def mix(q, u):
        s = q // CHUNKS
        for dx in (1, 3, 2):
            rt_copy(q, u, dx).wait_recv()

        def weights(k, low, high):
            return jnp.concatenate(
                [mixw[s, k, 0, low:high][:, 0:64], mixw[s, k, 1, low:high][:, 0:64]], axis=0
            )

        if u == 2:
            def body(at):
                rows = rbl[q, :, pl.ds(at, 128)]
                for k, base in ((2, 0), (3, FOLD)):
                    value = dot(weights(k, 96, 128), rows)
                    ct[q, 96:128, pl.ds(base + at, 128)] = value[0:32] + value[32:64]
            tiles(FOLD, 128, body)
        else:
            low, high, shared = (48, 112, 96) if u == 1 else (0, 64, 48)

            def body(at):
                both = dot(weights(u, low, high), rb[q, u, :, pl.ds(at, 256)])
                value = both[0:64] + both[64:128]
                ct[q, low:shared, pl.ds(at, 256)] = value[0:shared - low]
                ct[q, shared:high, pl.ds(at, 256)] = ct[q, shared:high, pl.ds(at, 256)] + value[shared - low:]
            tiles(COLS, 256, body)

    def gathered(q, slot):
        total = ct[q, ROWS * slot:ROWS * (slot + 1)]
        for i in children(q % CHUNKS, slot):
            rs_copy(q, i).wait_recv()
            total = total + rsr[q, ROWS * i:ROWS * (i + 1)].astype(F32)
        return total

    def reduce(q, slot):
        rss[q, ROWS * slot:ROWS * (slot + 1)] = gathered(q, slot).astype(BF16)
        start(rs_copy(q, slot))

    def finish(q):
        s, c = q // CHUNKS, q % CHUNKS
        total = gathered(q, 0) + state[s][:, c * COLS:(c + 1) * COLS].astype(F32)
        outs[s][0, :, c * COLS:(c + 1) * COLS] = total.astype(BF16)

    first, second = range(CHUNKS), range(CHUNKS, ITEMS)

    y_start(0)
    y_start(1)
    for i in range(1, NZ):
        start(meta_copy(i))
    norm(0)
    for q in first:
        z_send(q, 0)
    norm(1)
    plan()

    def step(items, slots):
        for q in items:
            for slot in slots:
                z_forward(q, slot)

    step(first, (1, 2))
    step(first, (3, 4))
    for q in second:
        z_send(q, 0)
    for q in first:
        select(q, 0)
    step(first, (5, 6))
    for q in first:
        select(q, 1)
    step(second, (1, 2))
    step(first, (7,))
    for q in first:
        select(q, 2)
    step(second, (3, 4))
    for q in second:
        select(q, 0)
    for q in first:
        exchange(q, 0)
    step(second, (5, 6))
    for q in second:
        select(q, 1)
    for q in first:
        exchange(q, 1)
    step(second, (7,))
    for q in second:
        select(q, 2)
    for q in first:
        exchange(q, 2)
    loads[0].wait()
    loads[1].wait()
    for q in first:
        gate_up(q)
    activate(0)
    loads[2].wait()
    for q in first:
        down(q)
    for q in first:
        send_back(q)
    for u in range(3):
        for q in second:
            exchange(q, u)
    for q in second:
        gate_up(q)
    activate(1)
    for q in second:
        down(q)
    for q in second:
        send_back(q)
    for q in first:
        mix(q, 2)
        reduce(q, 7)
        mix(q, 1)
        reduce(q, 6)
        mix(q, 0)
    for q in first:
        reduce(q, 5)
        reduce(q, 4)
    for q in second:
        mix(q, 2)
        reduce(q, 7)
    for q in first:
        reduce(q, 3)
        reduce(q, 2)
    for q in second:
        mix(q, 1)
        reduce(q, 6)
    for q in first:
        reduce(q, 1)
    for q in second:
        reduce(q, 5)
        reduce(q, 4)
    for q in second:
        mix(q, 0)
    for q in first:
        finish(q)
    for q in second:
        reduce(q, 3)
        reduce(q, 2)
    for q in second:
        reduce(q, 1)
    for q in second:
        finish(q)
    for copy in sent:
        copy.wait_send()


def body(*args):
    vmem = pl.BlockSpec(memory_space=pltpu.VMEM)
    hbm = pl.BlockSpec(memory_space=pl.ANY)
    dma = pltpu.SemaphoreType.DMA
    q = ITEMS
    state = jax.ShapeDtypeStruct((1, ROWS, WIDTH), BF16)
    return pl.pallas_call(
        kernel,
        out_shape=(state, state),
        in_specs=[vmem] * 6 + [hbm] * 3,
        out_specs=(vmem, vmem),
        scratch_shapes=[
            pltpu.VMEM((WIDTH, 2 * HALF), BF16),
            pltpu.VMEM((HALF, WIDTH), BF16),
            pltpu.VMEM((2, ROWS, WIDTH), BF16),
            pltpu.VMEM((128, 128), BF16),
            pltpu.VMEM((2, 4, 64, 128), BF16),
            pltpu.VMEM((2, 4, 2, 128, 128), BF16),
            pltpu.VMEM((q, 128, COLS), BF16),
            pltpu.VMEM((q, 2, 64, COLS), BF16),
            pltpu.VMEM((q, 64, FOLD), BF16),
            pltpu.VMEM((q, 320, COLS), BF16),
            pltpu.VMEM((q, 2, 64, FOLD), BF16),
            pltpu.VMEM((320, 2 * HALF), F32),
            pltpu.VMEM((2, 320, HALF), BF16),
            pltpu.VMEM((q, 160, COLS), F32),
            pltpu.VMEM((q, 160, COLS), BF16),
            pltpu.VMEM((q, 160, COLS), BF16),
            pltpu.VMEM((q, 2, 64, COLS), BF16),
            pltpu.VMEM((q, 64, FOLD), BF16),
            pltpu.VMEM((q, 2, 64, COLS), BF16),
            pltpu.VMEM((q, 64, FOLD), BF16),
            pltpu.VMEM((q, 128, COLS), F32),
            pltpu.VMEM((q, 128, COLS), BF16),
            pltpu.VMEM((q, 128, COLS), BF16),
            dma((3,)),
            dma((2,)), dma((2,)),
            dma((NZ,)), dma((NZ,)),
            dma((q, NZ)), dma((q, NZ)),
            dma((q, 3, NX)), dma((q, 3, NX)),
            dma((q, 3)), dma((q, 3)),
            dma((q,)), dma((q,)),
            dma((q, 3, NX)), dma((q, 3, NX)),
            dma((q, NZ)), dma((q, NZ)),
        ],
        compiler_params=pltpu.CompilerParams(
            collective_id=0, has_side_effects=True, vmem_limit_bytes=60 * 2**20
        ),
        name="routed_layer",
    )(*args)


def solution(mesh):
    states = P("section", "expert", None)
    routes = P(None, None, "expert", None)
    weights = P("section", "expert", None, None)
    return jax.shard_map(
        body,
        mesh=mesh,
        in_specs=(states, states, routes, routes, routes, routes, weights, weights, weights),
        out_specs=(states, states),
        check_vma=False,
    )
```

```python
import functools

import jax
import jax.numpy as jnp
from jax import lax
from jax.experimental import pallas as pl
from jax.experimental.pallas import tpu as pltpu
from jax.sharding import PartitionSpec as P

MESH = pl.DeviceIdType.MESH
F32 = jnp.float32
BF16 = jnp.bfloat16

WIDTH = 3584
HALF = 512
ROWS = 16
TOP = 8
CAP = 5
CHUNKS = 2
COLS = WIDTH // CHUNKS
FOLD = COLS // 2
ITEMS = 2 * CHUNKS
NX = 4
NZ = 8
OFFSETS = (0, 1, -1, 2, -2, 3, -3, 4)


RING = ((None, 0, 0, 1, 2, 3, 4, 5), (None, 0, 0, 1, 2, 3, 4, 6))
TREE = (None, 0, 0, 0, 0, 3, 4, 3)

ORDER = (
    ("first", ((0,), (2,),)),
    ("plan", ((),)),
    ("first", ((1,), (3,),)),
    ("forward", ((0, 1), (0, 2), (0, 3),)),
    ("select", ((0, 0),)),
    ("forward", ((0, 4), (2, 1), (2, 2), (1, 1), (1, 2),)),
    ("exchange", ((0, 0),)),
    ("forward", ((1, 3),)),
    ("select", ((1, 0),)),
    ("forward", ((1, 4), (3, 1), (3, 2), (0, 5), (0, 6),)),
    ("select", ((0, 1),)),
    ("forward", ((2, 4), (0, 7),)),
    ("select", ((0, 2),)),
    ("forward", ((1, 6),)),
    ("exchange", ((1, 0),)),
    ("forward", ((2, 3),)),
    ("select", ((2, 0),)),
    ("forward", ((3, 4), (1, 5),)),
    ("select", ((1, 1),)),
    ("forward", ((2, 6),)),
    ("exchange", ((0, 1), (0, 2),)),
    ("gate_up", ((0, 0),)),
    ("forward", ((1, 7),)),
    ("select", ((1, 2),)),
    ("forward", ((3, 6),)),
    ("gate_up", ((0, 1),)),
    ("forward", ((3, 3),)),
    ("select", ((3, 0),)),
    ("exchange", ((2, 0),)),
    ("forward", ((2, 5),)),
    ("select", ((2, 1),)),
    ("exchange", ((1, 1),)),
    ("forward", ((3, 7),)),
    ("exchange", ((1, 2),)),
    ("forward", ((3, 5),)),
    ("select", ((3, 1), (3, 2),)),
    ("gate_up", ((1, 0),)),
    ("forward", ((2, 7),)),
    ("select", ((2, 2),)),
    ("gate_up", ((1, 1),)),
    ("exchange", ((3, 0),)),
    ("activate", ((0,),)),
    ("down", ((0, 0), (0, 1), (1, 0), (1, 1),)),
    ("exchange", ((2, 1),)),
    ("send_back", ((0, 2), (0, 0), (0, 1), (1, 2), (1, 0), (1, 1),)),
    ("exchange", ((3, 1), (3, 2), (2, 2),)),
    ("gate_up", ((2, 0),)),
    ("mix", ((0, 2),)),
    ("reduce", ((0, 7),)),
    ("gate_up", ((2, 1), (3, 0), (3, 1),)),
    ("activate", ((1,),)),
    ("down", ((2, 0), (2, 1), (3, 0), (3, 1),)),
    ("mix", ((0, 1),)),
    ("reduce", ((0, 5), (0, 6),)),
    ("mix", ((0, 0),)),
    ("send_back", ((2, 2), (2, 0),)),
    ("mix", ((1, 2),)),
    ("reduce", ((1, 7),)),
    ("send_back", ((2, 1), (3, 2), (3, 0), (3, 1),)),
    ("reduce", ((0, 3), (0, 4),)),
    ("mix", ((1, 1),)),
    ("reduce", ((1, 5), (1, 6),)),
    ("mix", ((1, 0),)),
    ("reduce", ((0, 1), (0, 2),)),
    ("mix", ((2, 2),)),
    ("reduce", ((2, 7), (1, 3), (1, 4),)),
    ("finish", ((0,),)),
    ("mix", ((2, 1),)),
    ("reduce", ((2, 5), (2, 6),)),
    ("mix", ((2, 0), (3, 2),)),
    ("reduce", ((1, 1), (1, 2), (3, 7), (2, 3), (2, 4),)),
    ("finish", ((1,),)),
    ("mix", ((3, 1),)),
    ("reduce", ((3, 5), (3, 6),)),
    ("mix", ((3, 0),)),
    ("reduce", ((3, 1), (3, 2), (2, 2), (2, 1), (3, 3), (3, 4),)),
    ("finish", ((2,), (3,),)),
)
DIRECT_OUT = (0, 1)
DIRECT_BACK = (3,)


def out_parents(q):
    return TREE if q in DIRECT_OUT else RING[q % 2]


def back_parents(q):
    return TREE if q in DIRECT_BACK else RING[q % 2]


def below(parents, slot):
    return [i for i in range(NZ) if parents[i] == slot]


def tiles(width, step, body):
    @pl.loop(0, width // step)
    def _(j):
        body(pl.multiple_of(j * step, step))


def dot(a, b):
    return jnp.dot(a, b, preferred_element_type=F32)


def kernel(
    tok_a, tok_b, ids_a, ids_b, gates_a, gates_b, gate_hbm, up_hbm, down_hbm,
    out_a, out_b,
    wgu, wdn, state, near, meta, sel, mixw, xg, snd, sndl, xs, fold, acc, hid, yo, yx, yr,
    ret, retl, rb, rbl, ct, rss, rsr,
    w_sem, y_s, y_r, yn_s, yn_r, m_s, m_r, ag_s, ag_r, x_s, x_r, ex_s, ex_r, yx_s, yx_r, rt_s, rt_r, rs_s, rs_r,
):
    section = lax.axis_index("section")
    place = lax.axis_index("expert")
    z_at, x_at = place // NX, place % NX
    partner = (section + 1 - 2 * (section % 2), place)

    def along_y(layers):
        return ((section + 2 * layers + 8) % 8, place)

    def along_z(steps):
        return (section, ((z_at + steps + 2 * NZ) % NZ) * NX + x_at)

    def along_x(steps):
        return (section, z_at * NX + (x_at + steps + NX) % NX)

    tokens = (tok_a, tok_b)
    outs = (out_a, out_b)
    sent = []
    loaded = set()
    arrived = set()

    def remote(src, dst, send, recv, device):
        return pltpu.make_async_remote_copy(
            src_ref=src, dst_ref=dst, send_sem=send, recv_sem=recv, device_id=device, device_id_type=MESH
        )

    def start(copy):
        copy.start()
        sent.append(copy)

    def y_copy(s):
        return remote(tokens[s].at[0], state.at[s], y_s.at[s], y_r.at[s], along_y(1 if s == 0 else -1))

    def yn_copy(q):
        return remote(
            near.at[q], xg.at[q, pl.ds(0, ROWS)], yn_s.at[q], yn_r.at[q], along_y(1 if q < CHUNKS else -1)
        )

    def meta_copy(i):
        return remote(
            meta.at[pl.ds(0, ROWS)], meta.at[pl.ds(ROWS * i, ROWS)], m_s.at[i], m_r.at[i], along_z(OFFSETS[i])
        )

    def ag_copy(q, i):
        p = out_parents(q)[i]
        return remote(
            xg.at[q, pl.ds(ROWS * p, ROWS)], xg.at[q, pl.ds(ROWS * i, ROWS)],
            ag_s.at[q, i], ag_r.at[q, i], along_z(OFFSETS[i] - OFFSETS[p]),
        )

    def x_copy(q, u, dx):
        sems = (x_s.at[q, u, dx], x_r.at[q, u, dx], along_x(dx))
        rows = pl.ds(16 * dx, 16)
        if u == 2:
            return remote(sndl.at[q, rows], fold.at[q, 0, rows], *sems)
        return remote(snd.at[q, u, rows], xs.at[q, pl.ds(64 * u + 16 * dx, 16)], *sems)

    def ex_copy(q, u):
        sems = (ex_s.at[q, u], ex_r.at[q, u], partner)
        if u == 2:
            return remote(fold.at[q, 0], fold.at[q, 1], *sems)
        return remote(xs.at[q, pl.ds(64 * u, 64)], xs.at[q, pl.ds(128 + 64 * u, 64)], *sems)

    def yx_copy(q):
        return remote(yx.at[q], yr.at[q], yx_s.at[q], yx_r.at[q], partner)

    def rt_copy(q, u, dx):
        sems = (rt_s.at[q, u, dx], rt_r.at[q, u, dx], along_x(-dx))
        rows = pl.ds(16 * dx, 16)
        if u == 2:
            return remote(retl.at[q, rows], rbl.at[q, rows], *sems)
        return remote(ret.at[q, u, rows], rb.at[q, u, rows], *sems)

    def rs_copy(q, i):
        p = back_parents(q)[i]
        rows = pl.ds(ROWS * i, ROWS)
        return remote(
            rss.at[q, rows], rsr.at[q, rows], rs_s.at[q, i], rs_r.at[q, i], along_z(OFFSETS[p] - OFFSETS[i])
        )

    loads = [
        pltpu.make_async_copy(gate_hbm.at[0, 0], wgu.at[:, pl.ds(0, HALF)], w_sem.at[0]),
        pltpu.make_async_copy(up_hbm.at[0, 0], wgu.at[:, pl.ds(HALF, HALF)], w_sem.at[1]),
        pltpu.make_async_copy(down_hbm.at[0, 0], wdn, w_sem.at[2]),
    ]
    for load in loads:
        load.start()

    barrier = pltpu.get_barrier_semaphore()
    friends = [along_y(1), along_y(-1), partner]
    friends += [along_z(OFFSETS[i]) for i in range(1, NZ)]
    friends += [along_x(dx) for dx in range(1, NX)]
    for friend in friends:
        pl.semaphore_signal(barrier, inc=1, device_id=friend, device_id_type=MESH)

    lane8 = lax.broadcasted_iota(jnp.int32, (TOP, 128), 1)
    row8 = lax.broadcasted_iota(jnp.int32, (TOP, 128), 0)
    block = jnp.zeros((ROWS, 128), F32)
    for s, (ids_ref, gates_ref) in enumerate(((ids_a, gates_a), (ids_b, gates_b))):
        ids = ids_ref[0, section].astype(F32).astype(BF16)
        gates = gates_ref[0, section]
        high = gates.astype(BF16)
        low = (gates - high.astype(F32)).astype(BF16)
        for j, part in enumerate((ids, high, low)):
            spot = jnp.where(lane8 == row8 + (24 * s + 8 * j), 1.0, 0.0).astype(BF16)
            block = block + lax.dot_general(part, spot, (((0,), (0,)), ((), ())), preferred_element_type=F32)
    meta[0:ROWS, :] = block.astype(BF16)

    def norm(s):
        values = tokens[s][0].astype(F32)
        scale = lax.rsqrt(jnp.mean(values * values, axis=-1, keepdims=True) + 1e-06)
        normed = (values * scale).astype(BF16)
        for c in range(CHUNKS):
            near[s * CHUNKS + c] = normed[:, c * COLS:(c + 1) * COLS]

    def first(q):
        yn_copy(q).wait_recv()
        z_send(q, 0)

    def z_send(q, slot):
        for i in below(out_parents(q), slot):
            start(ag_copy(q, i))

    def forward(q, slot):
        ag_copy(q, slot).wait_recv()
        z_send(q, slot)

    def plan():
        for i in range(1, NZ):
            meta_copy(i).wait_recv()
        table = meta[...].astype(F32).T
        lane = lax.broadcasted_iota(jnp.int32, (128, 128), 1)
        row = lax.broadcasted_iota(jnp.int32, (128, 128), 0)
        earlier = jnp.where((row // ROWS == lane // ROWS) & (row < lane), 1.0, 0.0).astype(BF16)
        first = (lax.broadcasted_iota(jnp.int32, (1, 128), 1) // ROWS) * CAP
        for s in range(2):
            ids_t, high_t, low_t = (table[24 * s + 8 * j:24 * s + 8 * j + 8] for j in range(3))
            named, highs, lows = [], [], []
            for dx in range(NX):
                expert_at = (z_at * NX + (x_at + dx) % NX).astype(F32)
                same = jnp.where(ids_t == expert_at, 1.0, 0.0)
                named.append(jnp.sum(same, axis=0, keepdims=True))
                highs.append(jnp.sum(same * high_t, axis=0, keepdims=True))
                lows.append(jnp.sum(same * low_t, axis=0, keepdims=True))
            stacked = jnp.concatenate(named + [jnp.zeros((8 - NX, 128), F32)], axis=0)
            before = dot(stacked.astype(BF16), earlier)
            for u, (least, most, shift) in enumerate(((0, 16, 0), (16, 32, 0), (32, 48, 0), (32, 48, 8))):
                picks = jnp.zeros((128, 128), F32)
                high_w = jnp.zeros((128, 128), F32)
                low_w = jnp.zeros((128, 128), F32)
                for dx in range(NX):
                    spot = first + before[dx:dx + 1].astype(jnp.int32)
                    here = (named[dx] > 0.5) & (spot >= least) & (spot < most)
                    target = jnp.where(here, spot - least + shift + 16 * dx, -1)
                    hit = row == target
                    picks = picks + jnp.where(hit, 1.0, 0.0)
                    high_w = high_w + jnp.where(hit, highs[dx], 0.0)
                    low_w = low_w + jnp.where(hit, lows[dx], 0.0)
                sel[s, u] = picks[0:64].astype(BF16)
                mixw[s, u, 0] = high_w.T.astype(BF16)
                mixw[s, u, 1] = low_w.T.astype(BF16)

    def select(q, u):
        s = q // CHUNKS
        if u == 2:
            value = dot(sel[s, 2], xg[q, :, 0:FOLD]) + dot(sel[s, 3], xg[q, :, FOLD:COLS])
            value = value.astype(BF16)
            fold[q, 0, 0:16] = value[0:16]
            sndl[q, 16:64] = value[16:64]
        else:
            depth = 64 if u == 0 else 112
            value = dot(sel[s, u][:, 0:depth], xg[q, 0:depth]).astype(BF16)
            xs[q, 64 * u:64 * u + 16] = value[0:16]
            snd[q, u, 16:64] = value[16:64]
        for dx in (2, 1, 3):
            start(x_copy(q, u, dx))

    def exchange(q, u):
        for dx in (1, 3, 2):
            x_copy(q, u, dx).wait_recv()
        start(ex_copy(q, u))

    def gate_up(q, part):
        c = q % CHUNKS
        if part == 0:
            unfold(q)
        wait_load(part)

        cols = pl.ds(part * HALF, HALF)
        value = dot(xs[q], wgu[c * COLS:(c + 1) * COLS, cols])
        acc[:, cols] = value if c == 0 else acc[:, cols] + value

    def unfold(q):
        for u in range(3):
            ex_copy(q, u).wait_recv()

        def body(at):
            for h in range(2):
                part = fold[q, h, :, pl.ds(at, 128)].astype(F32)
                left = jnp.concatenate([part[16 * dx:16 * dx + 8] for dx in range(NX)], axis=0)
                right = jnp.concatenate([part[16 * dx + 8:16 * dx + 16] for dx in range(NX)], axis=0)
                xs[q, 256 + 32 * h:288 + 32 * h, pl.ds(at, 128)] = left.astype(BF16)
                xs[q, 256 + 32 * h:288 + 32 * h, pl.ds(FOLD + at, 128)] = right.astype(BF16)
        tiles(FOLD, 128, body)

    def activate(s):
        def body(at):
            gate = acc[:, pl.ds(at, 128)]
            up = acc[:, pl.ds(HALF + at, 128)]
            hid[s, :, pl.ds(at, 128)] = (gate / (1.0 + jnp.exp(-gate)) * up).astype(BF16)
        tiles(HALF, 128, body)

    def down(q, part):
        s, c = q // CHUNKS, q % CHUNKS
        wait_load(2)
        for j in range(4 * part, 4 + 3 * part):
            value = dot(hid[s], wdn[:, c * COLS + 256 * j:c * COLS + 256 * (j + 1)])
            cols = pl.ds(256 * j, 256)
            yo[q, 0:128, cols] = value[0:128]
            yo[q, 128:160, cols] = value[256:288]
            yx[q, 0:128, cols] = value[128:256].astype(BF16)
            yx[q, 128:160, cols] = value[288:320].astype(BF16)
        if part == 1:
            start(yx_copy(q))

    def send_back(q, u):
        if u == 2:
            yx_copy(q).wait_recv()

            def body(at):
                near = yo[q, 128:160, pl.ds(at, 128)] + yr[q, 128:160, pl.ds(at, 128)].astype(F32)
                far = yo[q, 128:160, pl.ds(FOLD + at, 128)] + yr[q, 128:160, pl.ds(FOLD + at, 128)].astype(F32)
                for dx in range(NX):
                    both = jnp.concatenate([near[8 * dx:8 * dx + 8], far[8 * dx:8 * dx + 8]], axis=0).astype(BF16)
                    (rbl if dx == 0 else retl)[q, 16 * dx:16 * dx + 16, pl.ds(at, 128)] = both
            tiles(FOLD, 128, body)
        else:
            def body(at):
                rows = pl.ds(64 * u, 64)
                both = (yo[q, rows, pl.ds(at, 256)] + yr[q, rows, pl.ds(at, 256)].astype(F32)).astype(BF16)
                rb[q, u, 0:16, pl.ds(at, 256)] = both[0:16]
                ret[q, u, 16:64, pl.ds(at, 256)] = both[16:64]
            tiles(COLS, 256, body)
        for dx in (2, 1, 3):
            start(rt_copy(q, u, dx))

    def mix(q, u):
        s = q // CHUNKS
        for dx in (1, 3, 2):
            rt_copy(q, u, dx).wait_recv()

        def weights(k, low, high):
            return jnp.concatenate(
                [mixw[s, k, 0, low:high][:, 0:64], mixw[s, k, 1, low:high][:, 0:64]], axis=0
            )

        if u == 2:
            for k, base in ((2, 0), (3, FOLD)):
                value = dot(weights(k, 96, 128), rbl[q])
                ct[q, 96:128, base:base + FOLD] = value[0:32] + value[32:64]
        else:
            low, high, shared = (48, 112, 96) if u == 1 else (0, 64, 48)
            for base in (0, FOLD):
                both = dot(weights(u, low, high), rb[q, u, :, base:base + FOLD])
                value = both[0:64] + both[64:128]
                ct[q, low:shared, base:base + FOLD] = value[0:shared - low]
                ct[q, shared:high, base:base + FOLD] = ct[q, shared:high, base:base + FOLD] + value[shared - low:]

    def gathered(q, slot):
        total = ct[q, ROWS * slot:ROWS * (slot + 1)]
        for i in below(back_parents(q), slot):
            rs_copy(q, i).wait_recv()
            total = total + rsr[q, ROWS * i:ROWS * (i + 1)].astype(F32)
        return total

    def reduce(q, slot):
        rss[q, ROWS * slot:ROWS * (slot + 1)] = gathered(q, slot).astype(BF16)
        start(rs_copy(q, slot))

    def finish(q):
        s, c = q // CHUNKS, q % CHUNKS
        if s not in arrived:
            y_copy(s).wait_recv()
            arrived.add(s)
        total = gathered(q, 0) + state[s][:, c * COLS:(c + 1) * COLS].astype(F32)
        outs[s][0, :, c * COLS:(c + 1) * COLS] = total.astype(BF16)

    def wait_load(i):
        if i not in loaded:
            loads[i].wait()
            loaded.add(i)

    norm(0)
    norm(1)
    pl.semaphore_wait(barrier, len(friends))
    for q in range(ITEMS):
        start(yn_copy(q))
    for i in range(1, NZ):
        start(meta_copy(i))
    for s in range(2):
        start(y_copy(s))
    known = dict(
        first=first, plan=plan, forward=forward, select=select, exchange=exchange, gate_up=gate_up,
        activate=activate, down=down, send_back=send_back, mix=mix, reduce=reduce, finish=finish,
    )
    steps = [functools.partial(known[name], *which) for name, turns in ORDER for which in turns]
    for step in steps:
        step()
    for copy in sent:
        copy.wait_send()


def hand_over(a_ref, b_ref, out_a, out_b, sems):
    copies = [
        pltpu.make_async_copy(a_ref, out_a, sems.at[0]),
        pltpu.make_async_copy(b_ref, out_b, sems.at[1]),
    ]
    for copy in copies:
        copy.start()
    for copy in copies:
        copy.wait()


def layer(*args):
    vmem = pl.BlockSpec(memory_space=pltpu.VMEM)
    hbm = pl.BlockSpec(memory_space=pl.ANY)
    dma = pltpu.SemaphoreType.DMA
    q = ITEMS
    state = jax.ShapeDtypeStruct((1, ROWS, WIDTH), BF16)
    return pl.pallas_call(
        kernel,
        out_shape=(state, state),
        in_specs=[vmem] * 6 + [hbm] * 3,
        out_specs=(vmem, vmem),
        scratch_shapes=[
            pltpu.VMEM((WIDTH, 2 * HALF), BF16),
            pltpu.VMEM((HALF, WIDTH), BF16),
            pltpu.VMEM((2, ROWS, WIDTH), BF16),
            pltpu.VMEM((q, ROWS, COLS), BF16),
            pltpu.VMEM((128, 128), BF16),
            pltpu.VMEM((2, 4, 64, 128), BF16),
            pltpu.VMEM((2, 4, 2, 128, 128), BF16),
            pltpu.VMEM((q, 128, COLS), BF16),
            pltpu.VMEM((q, 2, 64, COLS), BF16),
            pltpu.VMEM((q, 64, FOLD), BF16),
            pltpu.VMEM((q, 320, COLS), BF16),
            pltpu.VMEM((q, 2, 64, FOLD), BF16),
            pltpu.VMEM((320, 2 * HALF), F32),
            pltpu.VMEM((2, 320, HALF), BF16),
            pltpu.VMEM((q, 160, COLS), F32),
            pltpu.VMEM((q, 160, COLS), BF16),
            pltpu.VMEM((q, 160, COLS), BF16),
            pltpu.VMEM((q, 2, 64, COLS), BF16),
            pltpu.VMEM((q, 64, FOLD), BF16),
            pltpu.VMEM((q, 2, 64, COLS), BF16),
            pltpu.VMEM((q, 64, FOLD), BF16),
            pltpu.VMEM((q, 128, COLS), F32),
            pltpu.VMEM((q, 128, COLS), BF16),
            pltpu.VMEM((q, 128, COLS), BF16),
            dma((3,)),
            dma((2,)), dma((2,)),
            dma((q,)), dma((q,)),
            dma((NZ,)), dma((NZ,)),
            dma((q, NZ)), dma((q, NZ)),
            dma((q, 3, NX)), dma((q, 3, NX)),
            dma((q, 3)), dma((q, 3)),
            dma((q,)), dma((q,)),
            dma((q, 3, NX)), dma((q, 3, NX)),
            dma((q, NZ)), dma((q, NZ)),
        ],
        compiler_params=pltpu.CompilerParams(
            collective_id=0, has_side_effects=True, vmem_limit_bytes=60 * 2**20
        ),
        name="routed_layer",
    )(*args)


def body(tok_a, tok_b, ids_a, ids_b, gates_a, gates_b, gate_proj, up_proj, down_proj):
    small = [jnp.transpose(v, (0, 1, 3, 2)) for v in (ids_a, ids_b, gates_a, gates_b)]
    done = layer(tok_a, tok_b, *small, gate_proj, up_proj, down_proj)
    return pl.pallas_call(
        hand_over,
        out_shape=tuple(jax.ShapeDtypeStruct(v.shape, v.dtype) for v in done),
        in_specs=[pl.BlockSpec(memory_space=pl.ANY)] * 2,
        out_specs=(pl.BlockSpec(memory_space=pl.ANY),) * 2,
        scratch_shapes=[pltpu.SemaphoreType.DMA((2,))],
        name="hand_over",
    )(*done)


def solution(mesh):
    states = P("section", "expert", None)
    routes = P(None, None, "expert", None)
    weights = P("section", "expert", None, None)
    return jax.shard_map(
        body,
        mesh=mesh,
        in_specs=(states, states, routes, routes, routes, routes, weights, weights, weights),
        out_specs=(states, states),
        check_vma=False,
    )
```

```python
import functools

import jax
import jax.numpy as jnp
from jax import lax
from jax.experimental import pallas as pl
from jax.experimental.pallas import tpu as pltpu
from jax.sharding import PartitionSpec as P

MESH = pl.DeviceIdType.MESH
F32 = jnp.float32
BF16 = jnp.bfloat16

WIDTH = 3584
HALF = 512
ROWS = 16
TOP = 8
CAP = 5
WIDTHS = (1024, 1280, 1280, 1280, 1280, 1024)
CHUNKS = len(WIDTHS) // 2
LOWS = tuple(sum(WIDTHS[q // CHUNKS * CHUNKS:q]) for q in range(len(WIDTHS)))
ITEMS = 2 * CHUNKS
NX = 4
NZ = 8
OFFSETS = (0, 1, -1, 2, -2, 3, -3, 4)


RING = ((None, 0, 0, 1, 2, 3, 4, 5), (None, 0, 0, 1, 2, 3, 4, 6))
TREE = (None, 0, 0, 0, 0, 3, 4, 3)
FAR = (None, None, None, None, None, 3, 4, 3)

UNITS = ((0, 16, 0), (16, 32, 0), (32, 48, 0), (32, 48, 8))

ORDER = (
    ("forward", ((0, 3),)),
    ("first", ((3,),)),
    ("plan", ((1,),)),
    ("first", ((5,), (4,),)),
    ("forward", ((0, 4),)),
    ("weigh", ((1,),)),
    ("forward", ((0, 1), (1, 4), (0, 2),)),
    ("plan", ((0,),)),
    ("first", ((0,),)),
    ("forward", ((3, 2), (0, 5),)),
    ("select", ((0, 0),)),
    ("forward", ((1, 3), (1, 1),)),
    ("first", ((1,),)),
    ("forward", ((1, 2),)),
    ("select", ((1, 0),)),
    ("first", ((2,),)),
    ("forward", ((0, 7), (0, 6),)),
    ("select", ((0, 2),)),
    ("forward", ((1, 6), (4, 2),)),
    ("select", ((0, 1),)),
    ("forward", ((5, 2), (5, 1),)),
    ("weigh", ((0,),)),
    ("exchange", ((0, 0),)),
    ("forward", ((3, 1), (1, 5),)),
    ("select", ((1, 1),)),
    ("forward", ((2, 2), (3, 4), (4, 1), (1, 7),)),
    ("select", ((1, 2),)),
    ("forward", ((2, 4), (2, 3), (2, 1),)),
    ("select", ((2, 0),)),
    ("forward", ((4, 4),)),
    ("exchange", ((0, 2),)),
    ("forward", ((3, 3),)),
    ("select", ((3, 0),)),
    ("forward", ((5, 3),)),
    ("exchange", ((0, 1),)),
    ("forward", ((3, 6), (4, 3), (2, 6), (5, 4), (2, 5),)),
    ("select", ((2, 1),)),
    ("forward", ((2, 7),)),
    ("select", ((2, 2),)),
    ("exchange", ((2, 0), (1, 2),)),
    ("select", ((5, 0),)),
    ("exchange", ((1, 1),)),
    ("gate_up", ((0, 0), (0, 1),)),
    ("forward", ((3, 5),)),
    ("exchange", ((1, 0),)),
    ("forward", ((3, 7),)),
    ("select", ((3, 2), (3, 1),)),
    ("exchange", ((3, 0),)),
    ("forward", ((5, 6), (4, 6), (4, 5),)),
    ("exchange", ((2, 1), (2, 2),)),
    ("select", ((4, 0),)),
    ("gate_up", ((1, 0), (1, 1),)),
    ("select", ((4, 1),)),
    ("gate_up", ((2, 0), (2, 1),)),
    ("activate", ((0,),)),
    ("down", ((2, 0),)),
    ("exchange", ((5, 0),)),
    ("forward", ((5, 5), (4, 7),)),
    ("select", ((4, 2),)),
    ("forward", ((5, 7),)),
    ("select", ((5, 2),)),
    ("down", ((1, 0),)),
    ("exchange", ((3, 1),)),
    ("select", ((5, 1),)),
    ("down", ((0, 0),)),
    ("send_back", ((2, 2), (2, 1),)),
    ("exchange", ((3, 2), (4, 1),)),
    ("send_back", ((1, 2), (0, 2),)),
    ("exchange", ((4, 0), (5, 2),)),
    ("send_back", ((1, 1),)),
    ("exchange", ((4, 2),)),
    ("gate_up", ((3, 0),)),
    ("exchange", ((5, 1),)),
    ("gate_up", ((3, 1),)),
    ("send_back", ((0, 1),)),
    ("gate_up", ((4, 0),)),
    ("send_back", ((1, 0),)),
    ("gate_up", ((4, 1),)),
    ("mix", ((2, 2),)),
    ("gate_up", ((5, 0), (5, 1),)),
    ("activate", ((1,),)),
    ("down", ((3, 0),)),
    ("reduce", ((2, 7),)),
    ("mix", ((0, 2),)),
    ("send_back", ((2, 0),)),
    ("mix", ((2, 1),)),
    ("reduce", ((2, 6),)),
    ("mix", ((1, 2),)),
    ("down", ((5, 0),)),
    ("reduce", ((0, 7),)),
    ("down", ((4, 0),)),
    ("mix", ((1, 1),)),
    ("reduce", ((1, 7), (1, 5),)),
    ("send_back", ((3, 2),)),
    ("mix", ((0, 1),)),
    ("send_back", ((3, 1),)),
    ("reduce", ((2, 5), (2, 4), (0, 6),)),
    ("send_back", ((4, 2), (0, 0), (5, 2), (4, 1),)),
    ("reduce", ((1, 6), (0, 5),)),
    ("mix", ((1, 0),)),
    ("reduce", ((1, 3),)),
    ("mix", ((2, 0),)),
    ("send_back", ((5, 1),)),
    ("mix", ((3, 2),)),
    ("reduce", ((3, 7), (2, 3),)),
    ("send_back", ((3, 0),)),
    ("mix", ((3, 1),)),
    ("reduce", ((3, 5), (0, 4),)),
    ("mix", ((4, 2),)),
    ("reduce", ((4, 7),)),
    ("send_back", ((4, 0),)),
    ("reduce", ((1, 4),)),
    ("send_back", ((5, 0),)),
    ("reduce", ((1, 1),)),
    ("mix", ((0, 0),)),
    ("reduce", ((0, 3), (3, 6),)),
    ("mix", ((5, 2),)),
    ("reduce", ((5, 7), (2, 2),)),
    ("mix", ((4, 1),)),
    ("reduce", ((4, 6), (4, 5), (1, 2), (2, 1), (0, 2),)),
    ("mix", ((5, 1),)),
    ("reduce", ((5, 5), (5, 6),)),
    ("mix", ((3, 0),)),
    ("reduce", ((3, 3), (3, 4), (0, 1), (4, 4),)),
    ("mix", ((4, 0),)),
    ("reduce", ((4, 3), (4, 1), (4, 2),)),
    ("mix", ((5, 0),)),
    ("reduce", ((5, 4), (5, 1), (5, 3), (3, 1),)),
    ("finish", ((1,),)),
    ("reduce", ((5, 2), (3, 2),)),
    ("finish", ((4,), (2,), (0,), (5,), (3,),)),
)
DIRECT_OUT = (0, 1, 2)
DIRECT_BACK = (5, 4)
FROM_FAR = (0, 1)


def stream(q):
    return q // CHUNKS


def width(q):
    return WIDTHS[q]


def cols(q, part=0, parts=1):
    size = width(q) // parts
    return pl.ds(LOWS[q] + part * size, size)


def half(q):
    return pl.ds(LOWS[q] // 2, width(q) // 2)


def out_parents(q):
    if q in FROM_FAR:
        return FAR
    return TREE if q in DIRECT_OUT else RING[q % 2]


def back_parents(q):
    return TREE if q in DIRECT_BACK else RING[q % 2]


def below(parents, slot):
    return [i for i in range(NZ) if parents[i] == slot]


def tiles(width, step, body):
    @pl.loop(0, width // step)
    def _(j):
        body(pl.multiple_of(j * step, step))


def dot(a, b):
    return jnp.dot(a, b, preferred_element_type=F32)


def kernel(
    tok_a, tok_b, ids_a, ids_b, gates_a, gates_b, gate_hbm, up_hbm, down_hbm,
    out_a, out_b,
    wgu, wdn, state, near, meta, table, sel, mixw, xg, snd, sndl, xs, fold, acc, hid, yo, yx, yr,
    ret, retl, rb, rbl, ct, rss, rsr,
    w_sem, y_s, y_r, yn_s, yn_r, m_s, m_r, ag_s, ag_r, x_s, x_r, ex_s, ex_r, yx_s, yx_r, rt_s, rt_r, rs_s, rs_r,
):
    section = lax.axis_index("section")
    place = lax.axis_index("expert")
    z_at, x_at = place // NX, place % NX
    partner = (section + 1 - 2 * (section % 2), place)

    def along_y(layers):
        return ((section + 2 * layers + 8) % 8, place)

    def along_z(steps):
        return (section, ((z_at + steps + 2 * NZ) % NZ) * NX + x_at)

    def along_x(steps):
        return (section, z_at * NX + (x_at + steps + NX) % NX)

    tokens = (tok_a, tok_b)
    outs = (out_a, out_b)
    sent = []
    loaded = set()
    arrived = set()
    arrived_meta = []

    def remote(src, dst, send, recv, device):
        return pltpu.make_async_remote_copy(
            src_ref=src, dst_ref=dst, send_sem=send, recv_sem=recv, device_id=device, device_id_type=MESH
        )

    def start(copy):
        copy.start()
        sent.append(copy)

    def y_copy(s):
        return remote(tokens[s].at[0], state.at[s], y_s.at[s], y_r.at[s], along_y(1 if s == 0 else -1))

    def ahead(q):
        return 1 if stream(q) == 0 else -1

    def yn_copy(q):
        return remote(
            near.at[stream(q), :, cols(q)], xg.at[stream(q), pl.ds(0, ROWS), cols(q)],
            yn_s.at[q], yn_r.at[q], along_y(ahead(q)),
        )

    def meta_copy(i):
        return remote(
            meta.at[pl.ds(0, ROWS)], meta.at[pl.ds(ROWS * i, ROWS)], m_s.at[i], m_r.at[i], along_z(OFFSETS[i])
        )

    def ag_copy(q, i):
        p, to = out_parents(q)[i], xg.at[stream(q), pl.ds(ROWS * i, ROWS), cols(q)]
        if p is None:
            device = (along_y(ahead(q))[0], along_z(OFFSETS[i])[1])
            return remote(near.at[stream(q), :, cols(q)], to, ag_s.at[q, i], ag_r.at[q, i], device)
        return remote(
            xg.at[stream(q), pl.ds(ROWS * p, ROWS), cols(q)], to,
            ag_s.at[q, i], ag_r.at[q, i], along_z(OFFSETS[i] - OFFSETS[p]),
        )

    def x_copy(q, u, dx):
        sems = (x_s.at[q, u, dx], x_r.at[q, u, dx], along_x(dx))
        rows, s = pl.ds(16 * dx, 16), stream(q)
        if u == 2:
            return remote(sndl.at[s, rows, half(q)], fold.at[s, 0, rows, half(q)], *sems)
        return remote(snd.at[s, u, rows, cols(q)], xs.at[s, pl.ds(64 * u + 16 * dx, 16), cols(q)], *sems)

    def ex_copy(q, u):
        sems, s = (ex_s.at[q, u], ex_r.at[q, u], partner), stream(q)
        if u == 2:
            return remote(fold.at[s, 0, :, half(q)], fold.at[s, 1, :, half(q)], *sems)
        return remote(xs.at[s, pl.ds(64 * u, 64), cols(q)], xs.at[s, pl.ds(128 + 64 * u, 64), cols(q)], *sems)

    def yx_copy(q):
        s = stream(q)
        return remote(yx.at[s, :, cols(q)], yr.at[s, :, cols(q)], yx_s.at[q], yx_r.at[q], partner)

    def rt_copy(q, u, dx):
        sems = (rt_s.at[q, u, dx], rt_r.at[q, u, dx], along_x(-dx))
        rows, s = pl.ds(16 * dx, 16), stream(q)
        if u == 2:
            return remote(retl.at[s, rows, half(q)], rbl.at[s, rows, half(q)], *sems)
        return remote(ret.at[s, u, rows, cols(q)], rb.at[s, u, rows, cols(q)], *sems)

    def rs_copy(q, i):
        p, s = back_parents(q)[i], stream(q)
        rows = pl.ds(ROWS * i, ROWS)
        return remote(
            rss.at[s, rows, cols(q)], rsr.at[s, rows, cols(q)],
            rs_s.at[q, i], rs_r.at[q, i], along_z(OFFSETS[p] - OFFSETS[i]),
        )

    loads = [
        pltpu.make_async_copy(gate_hbm.at[0, 0], wgu.at[:, pl.ds(0, HALF)], w_sem.at[0]),
        pltpu.make_async_copy(up_hbm.at[0, 0], wgu.at[:, pl.ds(HALF, HALF)], w_sem.at[1]),
        pltpu.make_async_copy(down_hbm.at[0, 0], wdn, w_sem.at[2]),
    ]
    for load in loads:
        load.start()

    barrier = pltpu.get_barrier_semaphore()
    friends = [along_y(1), along_y(-1), partner]
    if FROM_FAR:
        friends += [(along_y(y)[0], along_z(OFFSETS[i])[1]) for y in (1, -1) for i in range(1, 5)]
    friends += [along_z(OFFSETS[i]) for i in range(1, NZ)]
    friends += [along_x(dx) for dx in range(1, NX)]
    for friend in friends:
        pl.semaphore_signal(barrier, inc=1, device_id=friend, device_id_type=MESH)

    lane8 = lax.broadcasted_iota(jnp.int32, (TOP, 128), 1)
    row8 = lax.broadcasted_iota(jnp.int32, (TOP, 128), 0)
    block = jnp.zeros((ROWS, 128), F32)
    for s, (ids_ref, gates_ref) in enumerate(((ids_a, gates_a), (ids_b, gates_b))):
        ids = ids_ref[0, section].astype(F32).astype(BF16)
        gates = gates_ref[0, section]
        high = gates.astype(BF16)
        low = (gates - high.astype(F32)).astype(BF16)
        for j, part in enumerate((ids, high, low)):
            spot = jnp.where(lane8 == row8 + (24 * s + 8 * j), 1.0, 0.0).astype(BF16)
            block = block + lax.dot_general(part, spot, (((0,), (0,)), ((), ())), preferred_element_type=F32)
    meta[0:ROWS, :] = block.astype(BF16)

    def norm(s):
        values = tokens[s][0].astype(F32)
        scale = lax.rsqrt(jnp.mean(values * values, axis=-1, keepdims=True) + 1e-06)
        near[s] = (values * scale).astype(BF16)

    def first(q):
        yn_copy(q).wait_recv()
        z_send(q, 0)

    def z_send(q, slot):
        for i in below(out_parents(q), slot):
            start(ag_copy(q, i))

    def forward(q, slot):
        ag_copy(q, slot).wait_recv()
        z_send(q, slot)

    def spots(s):
        if not arrived_meta:
            arrived_meta.append(True)
            for i in range(1, NZ):
                meta_copy(i).wait_recv()
            table[...] = meta[...].astype(F32).T
        ids_t, high_t, low_t = (table[24 * s + 8 * j:24 * s + 8 * j + 8] for j in range(3))
        named, highs, lows = [], [], []
        for dx in range(NX):
            expert_at = (z_at * NX + (x_at + dx) % NX).astype(F32)
            same = jnp.where(ids_t == expert_at, 1.0, 0.0)
            named.append(jnp.sum(same, axis=0, keepdims=True))
            highs.append(jnp.sum(same * high_t, axis=0, keepdims=True))
            lows.append(jnp.sum(same * low_t, axis=0, keepdims=True))
        stacked = jnp.concatenate(named + [jnp.zeros((8 - NX, 128), F32)], axis=0)
        lane = lax.broadcasted_iota(jnp.int32, (128, 128), 1)
        row = lax.broadcasted_iota(jnp.int32, (128, 128), 0)
        earlier = jnp.where((row // ROWS == lane // ROWS) & (row < lane), 1.0, 0.0).astype(BF16)
        before = dot(stacked.astype(BF16), earlier).astype(jnp.int32)
        first = (lax.broadcasted_iota(jnp.int32, (1, 128), 1) // ROWS) * CAP
        rows = [jnp.where(named[dx] > 0.5, first + before[dx:dx + 1], -1) for dx in range(NX)]
        return rows, highs, lows

    def hits(spot, u, dx, count):
        least, most, shift = UNITS[u]
        target = jnp.where((spot >= least) & (spot < most), spot - least + shift + 16 * dx, -1)
        return lax.broadcasted_iota(jnp.int32, (count, 128), 0) == target

    def plan(s):
        rows, _, _ = spots(s)
        for u in range(4):
            picks = jnp.zeros((64, 128), F32)
            for dx in range(NX):
                picks = jnp.where(hits(rows[dx], u, dx, 64), 1.0, picks)
            sel[s, u] = picks.astype(BF16)

    def weigh(s):
        rows, highs, lows = spots(s)
        for u in range(4):
            high_w = jnp.zeros((128, 128), F32)
            low_w = jnp.zeros((128, 128), F32)
            for dx in range(NX):
                hit = hits(rows[dx], u, dx, 128)
                high_w = jnp.where(hit, highs[dx], high_w)
                low_w = jnp.where(hit, lows[dx], low_w)
            mixw[s, u, 0] = high_w.T.astype(BF16)
            mixw[s, u, 1] = low_w.T.astype(BF16)

    def select(q, u):
        s = stream(q)
        if u == 2:
            value = dot(sel[s, 2], xg[s, :, cols(q, 0, 2)]) + dot(sel[s, 3], xg[s, :, cols(q, 1, 2)])
            value = value.astype(BF16)
            fold[s, 0, 0:16, half(q)] = value[0:16]
            sndl[s, 16:64, half(q)] = value[16:64]
        else:
            depth = 64 if u == 0 else 112
            value = dot(sel[s, u][:, 0:depth], xg[s, 0:depth, cols(q)]).astype(BF16)
            xs[s, 64 * u:64 * u + 16, cols(q)] = value[0:16]
            snd[s, u, 16:64, cols(q)] = value[16:64]
        for dx in (2, 1, 3):
            start(x_copy(q, u, dx))

    def exchange(q, u):
        for dx in (1, 3, 2):
            x_copy(q, u, dx).wait_recv()
        start(ex_copy(q, u))

    def gate_up(q, part):
        s, c = stream(q), q % CHUNKS
        if part == 0:
            unfold(q)
        wait_load(part)
        side = pl.ds(part * HALF, HALF)
        value = dot(xs[s, :, cols(q)], wgu[cols(q), side])
        acc[:, side] = value if c == 0 else acc[:, side] + value

    def unfold(q):
        s = stream(q)
        for u in range(3):
            ex_copy(q, u).wait_recv()
        for h in range(2):
            part = fold[s, h, :, half(q)].astype(F32)
            left = jnp.concatenate([part[16 * dx:16 * dx + 8] for dx in range(NX)], axis=0)
            right = jnp.concatenate([part[16 * dx + 8:16 * dx + 16] for dx in range(NX)], axis=0)
            xs[s, 256 + 32 * h:288 + 32 * h, cols(q, 0, 2)] = left.astype(BF16)
            xs[s, 256 + 32 * h:288 + 32 * h, cols(q, 1, 2)] = right.astype(BF16)

    def activate(s):
        def body(at):
            gate = acc[:, pl.ds(at, 128)]
            up = acc[:, pl.ds(HALF + at, 128)]
            hid[s, :, pl.ds(at, 128)] = (gate / (1.0 + jnp.exp(-gate)) * up).astype(BF16)
        tiles(HALF, 128, body)

    def down(q, part):
        s = stream(q)
        wait_load(2)
        for j in range(width(q) // 256):
            at = pl.ds(LOWS[q] + 256 * j, 256)
            value = dot(hid[s], wdn[:, at])
            yo[s, 0:128, at] = value[0:128]
            yo[s, 128:160, at] = value[256:288]
            yx[s, 0:128, at] = value[128:256].astype(BF16)
            yx[s, 128:160, at] = value[288:320].astype(BF16)
        start(yx_copy(q))

    def send_back(q, u):
        s = stream(q)
        if u == 2:
            yx_copy(q).wait_recv()
            rows = pl.ds(128, 32)
            near_half, far_half = (
                yo[s, rows, cols(q, k, 2)] + yr[s, rows, cols(q, k, 2)].astype(F32) for k in range(2)
            )
            for dx in range(NX):
                part = slice(8 * dx, 8 * dx + 8)
                both = jnp.concatenate([near_half[part], far_half[part]], axis=0).astype(BF16)
                (rbl if dx == 0 else retl)[s, 16 * dx:16 * dx + 16, half(q)] = both
        else:
            rows = pl.ds(64 * u, 64)
            both = (yo[s, rows, cols(q)] + yr[s, rows, cols(q)].astype(F32)).astype(BF16)
            rb[s, u, 0:16, cols(q)] = both[0:16]
            ret[s, u, 16:64, cols(q)] = both[16:64]
        for dx in (2, 1, 3):
            start(rt_copy(q, u, dx))

    def mix(q, u):
        s = stream(q)
        for dx in (1, 3, 2):
            rt_copy(q, u, dx).wait_recv()

        def weights(k, low, high):
            return jnp.concatenate(
                [mixw[s, k, 0, low:high][:, 0:64], mixw[s, k, 1, low:high][:, 0:64]], axis=0
            )

        if u == 2:
            for k in range(2):
                value = dot(weights(2 + k, 96, 128), rbl[s, :, half(q)])
                ct[s, 96:128, cols(q, k, 2)] = value[0:32] + value[32:64]
        else:
            low, high, shared = (48, 112, 96) if u == 1 else (0, 64, 48)
            for k in range(2):
                at = cols(q, k, 2)
                both = dot(weights(u, low, high), rb[s, u, :, at])
                value = both[0:64] + both[64:128]
                ct[s, low:shared, at] = value[0:shared - low]
                ct[s, shared:high, at] = ct[s, shared:high, at] + value[shared - low:]

    def gathered(q, slot):
        s = stream(q)
        total = ct[s, ROWS * slot:ROWS * (slot + 1), cols(q)]
        for i in below(back_parents(q), slot):
            rs_copy(q, i).wait_recv()
            total = total + rsr[s, ROWS * i:ROWS * (i + 1), cols(q)].astype(F32)
        return total

    def reduce(q, slot):
        rss[stream(q), ROWS * slot:ROWS * (slot + 1), cols(q)] = gathered(q, slot).astype(BF16)
        start(rs_copy(q, slot))

    def finish(q):
        s = stream(q)
        if s not in arrived:
            y_copy(s).wait_recv()
            arrived.add(s)
        total = gathered(q, 0) + state[s, :, cols(q)].astype(F32)
        outs[s][0, :, cols(q)] = total.astype(BF16)

    def wait_load(i):
        if i not in loaded:
            loads[i].wait()
            loaded.add(i)

    norm(0)
    norm(1)
    pl.semaphore_wait(barrier, len(friends))
    for q in range(ITEMS):
        for i in (3, 4, 1, 2):
            if q in FROM_FAR:
                start(ag_copy(q, i))
        start(yn_copy(q))
        if q == 0:
            for i in range(1, NZ):
                start(meta_copy(i))
    for s in range(2):
        start(y_copy(s))
    known = dict(
        first=first, plan=plan, weigh=weigh, forward=forward, select=select, exchange=exchange, gate_up=gate_up,
        activate=activate, down=down, send_back=send_back, mix=mix, reduce=reduce, finish=finish,
    )
    steps = [functools.partial(known[name], *which) for name, turns in ORDER for which in turns]
    for step in steps:
        step()
    for copy in sent:
        copy.wait_send()


def hand_over(a_ref, b_ref, out_a, out_b):
    out_a[...] = a_ref[...]
    out_b[...] = b_ref[...]


def layer(*args):
    vmem = pl.BlockSpec(memory_space=pltpu.VMEM)
    hbm = pl.BlockSpec(memory_space=pl.ANY)
    dma = pltpu.SemaphoreType.DMA
    q = ITEMS
    state = jax.ShapeDtypeStruct((1, ROWS, WIDTH), BF16)
    return pl.pallas_call(
        kernel,
        out_shape=(state, state),
        in_specs=[vmem] * 6 + [hbm] * 3,
        out_specs=(vmem, vmem),
        scratch_shapes=[
            pltpu.VMEM((WIDTH, 2 * HALF), BF16),
            pltpu.VMEM((HALF, WIDTH), BF16),
            pltpu.VMEM((2, ROWS, WIDTH), BF16),
            pltpu.VMEM((2, ROWS, WIDTH), BF16),
            pltpu.VMEM((128, 128), BF16),
            pltpu.VMEM((128, 128), F32),
            pltpu.VMEM((2, 4, 64, 128), BF16),
            pltpu.VMEM((2, 4, 2, 128, 128), BF16),
            pltpu.VMEM((2, 128, WIDTH), BF16),
            pltpu.VMEM((2, 2, 64, WIDTH), BF16),
            pltpu.VMEM((2, 64, WIDTH // 2), BF16),
            pltpu.VMEM((2, 320, WIDTH), BF16),
            pltpu.VMEM((2, 2, 64, WIDTH // 2), BF16),
            pltpu.VMEM((320, 2 * HALF), F32),
            pltpu.VMEM((2, 320, HALF), BF16),
            pltpu.VMEM((2, 160, WIDTH), F32),
            pltpu.VMEM((2, 160, WIDTH), BF16),
            pltpu.VMEM((2, 160, WIDTH), BF16),
            pltpu.VMEM((2, 2, 64, WIDTH), BF16),
            pltpu.VMEM((2, 64, WIDTH // 2), BF16),
            pltpu.VMEM((2, 2, 64, WIDTH), BF16),
            pltpu.VMEM((2, 64, WIDTH // 2), BF16),
            pltpu.VMEM((2, 128, WIDTH), F32),
            pltpu.VMEM((2, 128, WIDTH), BF16),
            pltpu.VMEM((2, 128, WIDTH), BF16),
            dma((3,)),
            dma((2,)), dma((2,)),
            dma((q,)), dma((q,)),
            dma((NZ,)), dma((NZ,)),
            dma((q, NZ)), dma((q, NZ)),
            dma((q, 3, NX)), dma((q, 3, NX)),
            dma((q, 3)), dma((q, 3)),
            dma((q,)), dma((q,)),
            dma((q, 3, NX)), dma((q, 3, NX)),
            dma((q, NZ)), dma((q, NZ)),
        ],
        compiler_params=pltpu.CompilerParams(
            collective_id=0, has_side_effects=True, vmem_limit_bytes=60 * 2**20
        ),
        name="routed_layer",
    )(*args)


def body(tok_a, tok_b, ids_a, ids_b, gates_a, gates_b, gate_proj, up_proj, down_proj):
    small = [jnp.transpose(v, (0, 1, 3, 2)) for v in (ids_a, ids_b, gates_a, gates_b)]
    done = layer(tok_a, tok_b, *small, gate_proj, up_proj, down_proj)
    return pl.pallas_call(
        hand_over,
        out_shape=tuple(jax.ShapeDtypeStruct(v.shape, v.dtype) for v in done),
        name="hand_over",
    )(*done)


def solution(mesh):
    states = P("section", "expert", None)
    routes = P(None, None, "expert", None)
    weights = P("section", "expert", None, None)
    return jax.shard_map(
        body,
        mesh=mesh,
        in_specs=(states, states, routes, routes, routes, routes, weights, weights, weights),
        out_specs=(states, states),
        check_vma=False,
    )
```

```python
import functools

import jax
import jax.numpy as jnp
from jax import lax
from jax.experimental import pallas as pl
from jax.experimental.pallas import tpu as pltpu
from jax.sharding import PartitionSpec as P

MESH = pl.DeviceIdType.MESH
F32 = jnp.float32
BF16 = jnp.bfloat16

WIDTH = 3584
HALF = 512
ROWS = 16
TOP = 8
CAP = 5
WIDTHS = (1024, 1280, 1280, 1280, 1280, 1024)
CHUNKS = len(WIDTHS) // 2
LOWS = tuple(sum(WIDTHS[q // CHUNKS * CHUNKS:q]) for q in range(len(WIDTHS)))
ITEMS = 2 * CHUNKS
NX = 4
NZ = 8
OFFSETS = (0, 1, -1, 2, -2, 3, -3, 4)


RING = ((None, 0, 0, 1, 2, 3, 4, 5), (None, 0, 0, 1, 2, 3, 4, 6))
TREE = (None, 0, 0, 0, 0, 3, 4, 3)
FAR = (None, None, None, None, None, 3, 4, 3)

UNITS = ((0, 16, 0), (16, 32, 0), (32, 48, 0), (32, 48, 8))

ORDER = (
    ("forward", ((0, 3),)),
    ("first", ((3,),)),
    ("plan", ((1,),)),
    ("first", ((5,), (4,),)),
    ("forward", ((0, 4),)),
    ("weigh", ((1,),)),
    ("forward", ((0, 1), (1, 4), (0, 2),)),
    ("plan", ((0,),)),
    ("first", ((0,),)),
    ("forward", ((3, 2), (0, 5),)),
    ("select", ((0, 0),)),
    ("forward", ((1, 3), (1, 1),)),
    ("first", ((1,),)),
    ("forward", ((1, 2),)),
    ("select", ((1, 0),)),
    ("first", ((2,),)),
    ("forward", ((0, 7), (0, 6),)),
    ("select", ((0, 2),)),
    ("forward", ((1, 6), (4, 2),)),
    ("select", ((0, 1),)),
    ("forward", ((5, 2), (5, 1),)),
    ("weigh", ((0,),)),
    ("exchange", ((0, 0),)),
    ("forward", ((3, 1), (1, 5),)),
    ("select", ((1, 1),)),
    ("forward", ((2, 2), (3, 4), (4, 1), (1, 7),)),
    ("select", ((1, 2),)),
    ("forward", ((2, 4), (2, 3), (2, 1),)),
    ("select", ((2, 0),)),
    ("forward", ((4, 4),)),
    ("exchange", ((0, 2),)),
    ("forward", ((3, 3),)),
    ("select", ((3, 0),)),
    ("forward", ((5, 3),)),
    ("exchange", ((0, 1),)),
    ("forward", ((3, 6), (4, 3), (2, 6), (5, 4), (2, 5),)),
    ("select", ((2, 1),)),
    ("forward", ((2, 7),)),
    ("select", ((2, 2),)),
    ("exchange", ((2, 0), (1, 2),)),
    ("select", ((5, 0),)),
    ("exchange", ((1, 1),)),
    ("gate_up", ((0, 0), (0, 1),)),
    ("forward", ((3, 5),)),
    ("exchange", ((1, 0),)),
    ("forward", ((3, 7),)),
    ("select", ((3, 2), (3, 1),)),
    ("exchange", ((3, 0),)),
    ("forward", ((5, 6), (4, 6), (4, 5),)),
    ("exchange", ((2, 1), (2, 2),)),
    ("select", ((4, 0),)),
    ("gate_up", ((1, 0), (1, 1),)),
    ("select", ((4, 1),)),
    ("gate_up", ((2, 0), (2, 1),)),
    ("activate", ((0,),)),
    ("down", ((2, 0),)),
    ("exchange", ((5, 0),)),
    ("forward", ((5, 5), (4, 7),)),
    ("select", ((4, 2),)),
    ("forward", ((5, 7),)),
    ("select", ((5, 2),)),
    ("down", ((1, 0),)),
    ("exchange", ((3, 1),)),
    ("select", ((5, 1),)),
    ("down", ((0, 0),)),
    ("send_back", ((2, 2), (2, 1),)),
    ("exchange", ((3, 2), (4, 1),)),
    ("send_back", ((1, 2), (0, 2),)),
    ("exchange", ((4, 0), (5, 2),)),
    ("send_back", ((1, 1),)),
    ("exchange", ((4, 2),)),
    ("gate_up", ((3, 0),)),
    ("exchange", ((5, 1),)),
    ("gate_up", ((3, 1),)),
    ("send_back", ((0, 1),)),
    ("gate_up", ((4, 0),)),
    ("send_back", ((1, 0),)),
    ("gate_up", ((4, 1),)),
    ("mix", ((2, 2),)),
    ("gate_up", ((5, 0), (5, 1),)),
    ("activate", ((1,),)),
    ("down", ((3, 0),)),
    ("reduce", ((2, 7),)),
    ("mix", ((0, 2),)),
    ("send_back", ((2, 0),)),
    ("mix", ((2, 1),)),
    ("reduce", ((2, 6),)),
    ("mix", ((1, 2),)),
    ("down", ((5, 0),)),
    ("reduce", ((0, 7),)),
    ("down", ((4, 0),)),
    ("mix", ((1, 1),)),
    ("reduce", ((1, 7), (1, 5),)),
    ("send_back", ((3, 2),)),
    ("mix", ((0, 1),)),
    ("send_back", ((3, 1),)),
    ("reduce", ((2, 5), (2, 4), (0, 6),)),
    ("send_back", ((4, 2), (0, 0), (5, 2), (4, 1),)),
    ("reduce", ((1, 6), (0, 5),)),
    ("mix", ((1, 0),)),
    ("reduce", ((1, 3),)),
    ("mix", ((2, 0),)),
    ("send_back", ((5, 1),)),
    ("mix", ((3, 2),)),
    ("reduce", ((3, 7), (2, 3),)),
    ("send_back", ((3, 0),)),
    ("mix", ((3, 1),)),
    ("reduce", ((3, 5), (0, 4),)),
    ("mix", ((4, 2),)),
    ("reduce", ((4, 7),)),
    ("send_back", ((4, 0),)),
    ("reduce", ((1, 4),)),
    ("send_back", ((5, 0),)),
    ("reduce", ((1, 1),)),
    ("mix", ((0, 0),)),
    ("reduce", ((0, 3), (3, 6),)),
    ("mix", ((5, 2),)),
    ("reduce", ((5, 7), (2, 2),)),
    ("mix", ((4, 1),)),
    ("reduce", ((4, 6), (4, 5), (1, 2), (2, 1), (0, 2),)),
    ("mix", ((5, 1),)),
    ("reduce", ((5, 5), (5, 6),)),
    ("mix", ((3, 0),)),
    ("reduce", ((3, 3), (3, 4), (0, 1), (4, 4),)),
    ("mix", ((4, 0),)),
    ("reduce", ((4, 3), (4, 1), (4, 2),)),
    ("mix", ((5, 0),)),
    ("reduce", ((5, 4), (5, 1), (5, 3), (3, 1),)),
    ("finish", ((1,),)),
    ("reduce", ((5, 2), (3, 2),)),
    ("finish", ((4,), (2,), (0,), (5,), (3,),)),
)
DIRECT_OUT = (0, 1, 2)
DIRECT_BACK = (5, 4)
FROM_FAR = (0, 1)


def stream(q):
    return q // CHUNKS


def width(q):
    return WIDTHS[q]


def cols(q, part=0, parts=1):
    size = width(q) // parts
    return pl.ds(LOWS[q] + part * size, size)


def half(q):
    return pl.ds(LOWS[q] // 2, width(q) // 2)


def out_parents(q):
    if q in FROM_FAR:
        return FAR
    return TREE if q in DIRECT_OUT else RING[q % 2]


def back_parents(q):
    return TREE if q in DIRECT_BACK else RING[q % 2]


def below(parents, slot):
    return [i for i in range(NZ) if parents[i] == slot]


def tiles(width, step, body):
    @pl.loop(0, width // step)
    def _(j):
        body(pl.multiple_of(j * step, step))


def dot(a, b):
    return jnp.dot(a, b, preferred_element_type=F32)


def kernel(
    tok_a, tok_b, ids_a, ids_b, gates_a, gates_b, gate_hbm, up_hbm, down_hbm,
    out_a, out_b,
    ended, wgu, wdn, state, near, meta, table, sel, mixw, xg, snd, sndl, xs, fold, acc, hid, yo, yx, yr,
    ret, retl, rb, rbl, ct, rss, rsr,
    out_sem, w_sem, y_s, y_r, yn_s, yn_r, m_s, m_r, ag_s, ag_r, x_s, x_r, ex_s, ex_r, yx_s, yx_r, rt_s, rt_r, rs_s, rs_r,
):
    section = lax.axis_index("section")
    place = lax.axis_index("expert")
    z_at, x_at = place // NX, place % NX
    partner = (section + 1 - 2 * (section % 2), place)

    def along_y(layers):
        return ((section + 2 * layers + 8) % 8, place)

    def along_z(steps):
        return (section, ((z_at + steps + 2 * NZ) % NZ) * NX + x_at)

    def along_x(steps):
        return (section, z_at * NX + (x_at + steps + NX) % NX)

    tokens = (tok_a, tok_b)
    outs = (out_a, out_b)
    sent = []
    loaded = set()
    arrived = set()
    writes = []
    arrived_meta = []

    def remote(src, dst, send, recv, device):
        return pltpu.make_async_remote_copy(
            src_ref=src, dst_ref=dst, send_sem=send, recv_sem=recv, device_id=device, device_id_type=MESH
        )

    def start(copy):
        copy.start()
        sent.append(copy)

    def y_copy(s):
        return remote(tokens[s].at[0], state.at[s], y_s.at[s], y_r.at[s], along_y(1 if s == 0 else -1))

    def ahead(q):
        return 1 if stream(q) == 0 else -1

    def yn_copy(q):
        return remote(
            near.at[stream(q), :, cols(q)], xg.at[stream(q), pl.ds(0, ROWS), cols(q)],
            yn_s.at[q], yn_r.at[q], along_y(ahead(q)),
        )

    def meta_copy(i):
        return remote(
            meta.at[pl.ds(0, ROWS)], meta.at[pl.ds(ROWS * i, ROWS)], m_s.at[i], m_r.at[i], along_z(OFFSETS[i])
        )

    def ag_copy(q, i):
        p, to = out_parents(q)[i], xg.at[stream(q), pl.ds(ROWS * i, ROWS), cols(q)]
        if p is None:
            device = (along_y(ahead(q))[0], along_z(OFFSETS[i])[1])
            return remote(near.at[stream(q), :, cols(q)], to, ag_s.at[q, i], ag_r.at[q, i], device)
        return remote(
            xg.at[stream(q), pl.ds(ROWS * p, ROWS), cols(q)], to,
            ag_s.at[q, i], ag_r.at[q, i], along_z(OFFSETS[i] - OFFSETS[p]),
        )

    def x_copy(q, u, dx):
        sems = (x_s.at[q, u, dx], x_r.at[q, u, dx], along_x(dx))
        rows, s = pl.ds(16 * dx, 16), stream(q)
        if u == 2:
            return remote(sndl.at[s, rows, half(q)], fold.at[s, 0, rows, half(q)], *sems)
        return remote(snd.at[s, u, rows, cols(q)], xs.at[s, pl.ds(64 * u + 16 * dx, 16), cols(q)], *sems)

    def ex_copy(q, u):
        sems, s = (ex_s.at[q, u], ex_r.at[q, u], partner), stream(q)
        if u == 2:
            return remote(fold.at[s, 0, :, half(q)], fold.at[s, 1, :, half(q)], *sems)
        return remote(xs.at[s, pl.ds(64 * u, 64), cols(q)], xs.at[s, pl.ds(128 + 64 * u, 64), cols(q)], *sems)

    def yx_copy(q):
        s = stream(q)
        return remote(yx.at[s, :, cols(q)], yr.at[s, :, cols(q)], yx_s.at[q], yx_r.at[q], partner)

    def rt_copy(q, u, dx):
        sems = (rt_s.at[q, u, dx], rt_r.at[q, u, dx], along_x(-dx))
        rows, s = pl.ds(16 * dx, 16), stream(q)
        if u == 2:
            return remote(retl.at[s, rows, half(q)], rbl.at[s, rows, half(q)], *sems)
        return remote(ret.at[s, u, rows, cols(q)], rb.at[s, u, rows, cols(q)], *sems)

    def rs_copy(q, i):
        p, s = back_parents(q)[i], stream(q)
        rows = pl.ds(ROWS * i, ROWS)
        return remote(
            rss.at[s, rows, cols(q)], rsr.at[s, rows, cols(q)],
            rs_s.at[q, i], rs_r.at[q, i], along_z(OFFSETS[p] - OFFSETS[i]),
        )

    loads = [
        pltpu.make_async_copy(gate_hbm.at[0, 0], wgu.at[:, pl.ds(0, HALF)], w_sem.at[0]),
        pltpu.make_async_copy(up_hbm.at[0, 0], wgu.at[:, pl.ds(HALF, HALF)], w_sem.at[1]),
        pltpu.make_async_copy(down_hbm.at[0, 0], wdn, w_sem.at[2]),
    ]
    for load in loads:
        load.start()

    barrier = pltpu.get_barrier_semaphore()
    friends = [along_y(1), along_y(-1), partner]
    if FROM_FAR:
        friends += [(along_y(y)[0], along_z(OFFSETS[i])[1]) for y in (1, -1) for i in range(1, 5)]
    friends += [along_z(OFFSETS[i]) for i in range(1, NZ)]
    friends += [along_x(dx) for dx in range(1, NX)]
    for friend in friends:
        pl.semaphore_signal(barrier, inc=1, device_id=friend, device_id_type=MESH)

    lane8 = lax.broadcasted_iota(jnp.int32, (TOP, 128), 1)
    row8 = lax.broadcasted_iota(jnp.int32, (TOP, 128), 0)
    block = jnp.zeros((ROWS, 128), F32)
    for s, (ids_ref, gates_ref) in enumerate(((ids_a, gates_a), (ids_b, gates_b))):
        ids = ids_ref[0, section].astype(F32).astype(BF16)
        gates = gates_ref[0, section]
        high = gates.astype(BF16)
        low = (gates - high.astype(F32)).astype(BF16)
        for j, part in enumerate((ids, high, low)):
            spot = jnp.where(lane8 == row8 + (24 * s + 8 * j), 1.0, 0.0).astype(BF16)
            block = block + lax.dot_general(part, spot, (((0,), (0,)), ((), ())), preferred_element_type=F32)
    meta[0:ROWS, :] = block.astype(BF16)

    def norm(s):
        values = tokens[s][0].astype(F32)
        scale = lax.rsqrt(jnp.mean(values * values, axis=-1, keepdims=True) + 1e-06)
        near[s] = (values * scale).astype(BF16)

    def first(q):
        yn_copy(q).wait_recv()
        z_send(q, 0)

    def z_send(q, slot):
        for i in below(out_parents(q), slot):
            start(ag_copy(q, i))

    def forward(q, slot):
        ag_copy(q, slot).wait_recv()
        z_send(q, slot)

    def spots(s):
        if not arrived_meta:
            arrived_meta.append(True)
            for i in range(1, NZ):
                meta_copy(i).wait_recv()
            table[...] = meta[...].astype(F32).T
        ids_t, high_t, low_t = (table[24 * s + 8 * j:24 * s + 8 * j + 8] for j in range(3))
        named, highs, lows = [], [], []
        for dx in range(NX):
            expert_at = (z_at * NX + (x_at + dx) % NX).astype(F32)
            same = jnp.where(ids_t == expert_at, 1.0, 0.0)
            named.append(jnp.sum(same, axis=0, keepdims=True))
            highs.append(jnp.sum(same * high_t, axis=0, keepdims=True))
            lows.append(jnp.sum(same * low_t, axis=0, keepdims=True))
        stacked = jnp.concatenate(named + [jnp.zeros((8 - NX, 128), F32)], axis=0)
        lane = lax.broadcasted_iota(jnp.int32, (128, 128), 1)
        row = lax.broadcasted_iota(jnp.int32, (128, 128), 0)
        earlier = jnp.where((row // ROWS == lane // ROWS) & (row < lane), 1.0, 0.0).astype(BF16)
        before = dot(stacked.astype(BF16), earlier).astype(jnp.int32)
        first = (lax.broadcasted_iota(jnp.int32, (1, 128), 1) // ROWS) * CAP
        rows = [jnp.where(named[dx] > 0.5, first + before[dx:dx + 1], -1) for dx in range(NX)]
        return rows, highs, lows

    def hits(spot, u, dx, count):
        least, most, shift = UNITS[u]
        target = jnp.where((spot >= least) & (spot < most), spot - least + shift + 16 * dx, -1)
        return lax.broadcasted_iota(jnp.int32, (count, 128), 0) == target

    def plan(s):
        rows, _, _ = spots(s)
        for u in range(4):
            picks = jnp.zeros((64, 128), F32)
            for dx in range(NX):
                picks = jnp.where(hits(rows[dx], u, dx, 64), 1.0, picks)
            sel[s, u] = picks.astype(BF16)

    def weigh(s):
        rows, highs, lows = spots(s)
        for u in range(4):
            high_w = jnp.zeros((128, 128), F32)
            low_w = jnp.zeros((128, 128), F32)
            for dx in range(NX):
                hit = hits(rows[dx], u, dx, 128)
                high_w = jnp.where(hit, highs[dx], high_w)
                low_w = jnp.where(hit, lows[dx], low_w)
            mixw[s, u, 0] = high_w.T.astype(BF16)
            mixw[s, u, 1] = low_w.T.astype(BF16)

    def select(q, u):
        s = stream(q)
        if u == 2:
            value = dot(sel[s, 2], xg[s, :, cols(q, 0, 2)]) + dot(sel[s, 3], xg[s, :, cols(q, 1, 2)])
            value = value.astype(BF16)
            fold[s, 0, 0:16, half(q)] = value[0:16]
            sndl[s, 16:64, half(q)] = value[16:64]
        else:
            depth = 64 if u == 0 else 112
            value = dot(sel[s, u][:, 0:depth], xg[s, 0:depth, cols(q)]).astype(BF16)
            xs[s, 64 * u:64 * u + 16, cols(q)] = value[0:16]
            snd[s, u, 16:64, cols(q)] = value[16:64]
        for dx in (2, 1, 3):
            start(x_copy(q, u, dx))

    def exchange(q, u):
        for dx in (1, 3, 2):
            x_copy(q, u, dx).wait_recv()
        start(ex_copy(q, u))

    def gate_up(q, part):
        s, c = stream(q), q % CHUNKS
        if part == 0:
            unfold(q)
        wait_load(part)
        side = pl.ds(part * HALF, HALF)
        value = dot(xs[s, :, cols(q)], wgu[cols(q), side])
        acc[:, side] = value if c == 0 else acc[:, side] + value

    def unfold(q):
        s = stream(q)
        for u in range(3):
            ex_copy(q, u).wait_recv()
        for h in range(2):
            part = fold[s, h, :, half(q)].astype(F32)
            left = jnp.concatenate([part[16 * dx:16 * dx + 8] for dx in range(NX)], axis=0)
            right = jnp.concatenate([part[16 * dx + 8:16 * dx + 16] for dx in range(NX)], axis=0)
            xs[s, 256 + 32 * h:288 + 32 * h, cols(q, 0, 2)] = left.astype(BF16)
            xs[s, 256 + 32 * h:288 + 32 * h, cols(q, 1, 2)] = right.astype(BF16)

    def activate(s):
        def body(at):
            gate = acc[:, pl.ds(at, 128)]
            up = acc[:, pl.ds(HALF + at, 128)]
            hid[s, :, pl.ds(at, 128)] = (gate / (1.0 + jnp.exp(-gate)) * up).astype(BF16)
        tiles(HALF, 128, body)

    def down(q, part):
        s = stream(q)
        wait_load(2)
        for j in range(width(q) // 256):
            at = pl.ds(LOWS[q] + 256 * j, 256)
            value = dot(hid[s], wdn[:, at])
            yo[s, 0:128, at] = value[0:128]
            yo[s, 128:160, at] = value[256:288]
            yx[s, 0:128, at] = value[128:256].astype(BF16)
            yx[s, 128:160, at] = value[288:320].astype(BF16)
        start(yx_copy(q))

    def send_back(q, u):
        s = stream(q)
        if u == 2:
            yx_copy(q).wait_recv()
            rows = pl.ds(128, 32)
            near_half, far_half = (
                yo[s, rows, cols(q, k, 2)] + yr[s, rows, cols(q, k, 2)].astype(F32) for k in range(2)
            )
            for dx in range(NX):
                part = slice(8 * dx, 8 * dx + 8)
                both = jnp.concatenate([near_half[part], far_half[part]], axis=0).astype(BF16)
                (rbl if dx == 0 else retl)[s, 16 * dx:16 * dx + 16, half(q)] = both
        else:
            rows = pl.ds(64 * u, 64)
            both = (yo[s, rows, cols(q)] + yr[s, rows, cols(q)].astype(F32)).astype(BF16)
            rb[s, u, 0:16, cols(q)] = both[0:16]
            ret[s, u, 16:64, cols(q)] = both[16:64]
        for dx in (2, 1, 3):
            start(rt_copy(q, u, dx))

    def mix(q, u):
        s = stream(q)
        for dx in (1, 3, 2):
            rt_copy(q, u, dx).wait_recv()

        def weights(k, low, high):
            return jnp.concatenate(
                [mixw[s, k, 0, low:high][:, 0:64], mixw[s, k, 1, low:high][:, 0:64]], axis=0
            )

        if u == 2:
            for k in range(2):
                value = dot(weights(2 + k, 96, 128), rbl[s, :, half(q)])
                ct[s, 96:128, cols(q, k, 2)] = value[0:32] + value[32:64]
        else:
            low, high, shared = (48, 112, 96) if u == 1 else (0, 64, 48)
            for k in range(2):
                at = cols(q, k, 2)
                both = dot(weights(u, low, high), rb[s, u, :, at])
                value = both[0:64] + both[64:128]
                ct[s, low:shared, at] = value[0:shared - low]
                ct[s, shared:high, at] = ct[s, shared:high, at] + value[shared - low:]

    def gathered(q, slot):
        s = stream(q)
        total = ct[s, ROWS * slot:ROWS * (slot + 1), cols(q)]
        for i in below(back_parents(q), slot):
            rs_copy(q, i).wait_recv()
            total = total + rsr[s, ROWS * i:ROWS * (i + 1), cols(q)].astype(F32)
        return total

    def reduce(q, slot):
        rss[stream(q), ROWS * slot:ROWS * (slot + 1), cols(q)] = gathered(q, slot).astype(BF16)
        start(rs_copy(q, slot))

    def finish(q):
        s = stream(q)
        if s not in arrived:
            y_copy(s).wait_recv()
            arrived.add(s)
        total = gathered(q, 0) + state[s, :, cols(q)].astype(F32)
        ended[s, :, cols(q)] = total.astype(BF16)
        write = pltpu.make_async_copy(ended.at[s, :, cols(q)], outs[s].at[0, :, cols(q)], out_sem.at[q])
        write.start()
        writes.append(write)

    def wait_load(i):
        if i not in loaded:
            loads[i].wait()
            loaded.add(i)

    norm(0)
    norm(1)
    pl.semaphore_wait(barrier, len(friends))
    for q in range(ITEMS):
        for i in (3, 4, 1, 2):
            if q in FROM_FAR:
                start(ag_copy(q, i))
        start(yn_copy(q))
        if q == 0:
            for i in range(1, NZ):
                start(meta_copy(i))
    for s in range(2):
        start(y_copy(s))
    known = dict(
        first=first, plan=plan, weigh=weigh, forward=forward, select=select, exchange=exchange, gate_up=gate_up,
        activate=activate, down=down, send_back=send_back, mix=mix, reduce=reduce, finish=finish,
    )
    steps = [functools.partial(known[name], *which) for name, turns in ORDER for which in turns]
    for step in steps:
        step()
    for copy in sent:
        copy.wait_send()
    for write in writes:
        write.wait()


def hand_over(a_ref, b_ref, out_a, out_b):
    out_a[...] = a_ref[...]
    out_b[...] = b_ref[...]


def layer(*args):
    vmem = pl.BlockSpec(memory_space=pltpu.VMEM)
    hbm = pl.BlockSpec(memory_space=pl.ANY)
    dma = pltpu.SemaphoreType.DMA
    q = ITEMS
    state = jax.ShapeDtypeStruct((1, ROWS, WIDTH), BF16)
    return pl.pallas_call(
        kernel,
        out_shape=(state, state),
        in_specs=[vmem] * 6 + [hbm] * 3,
        out_specs=(hbm, hbm),
        scratch_shapes=[
            pltpu.VMEM((2, ROWS, WIDTH), BF16),
            pltpu.VMEM((WIDTH, 2 * HALF), BF16),
            pltpu.VMEM((HALF, WIDTH), BF16),
            pltpu.VMEM((2, ROWS, WIDTH), BF16),
            pltpu.VMEM((2, ROWS, WIDTH), BF16),
            pltpu.VMEM((128, 128), BF16),
            pltpu.VMEM((128, 128), F32),
            pltpu.VMEM((2, 4, 64, 128), BF16),
            pltpu.VMEM((2, 4, 2, 128, 128), BF16),
            pltpu.VMEM((2, 128, WIDTH), BF16),
            pltpu.VMEM((2, 2, 64, WIDTH), BF16),
            pltpu.VMEM((2, 64, WIDTH // 2), BF16),
            pltpu.VMEM((2, 320, WIDTH), BF16),
            pltpu.VMEM((2, 2, 64, WIDTH // 2), BF16),
            pltpu.VMEM((320, 2 * HALF), F32),
            pltpu.VMEM((2, 320, HALF), BF16),
            pltpu.VMEM((2, 160, WIDTH), F32),
            pltpu.VMEM((2, 160, WIDTH), BF16),
            pltpu.VMEM((2, 160, WIDTH), BF16),
            pltpu.VMEM((2, 2, 64, WIDTH), BF16),
            pltpu.VMEM((2, 64, WIDTH // 2), BF16),
            pltpu.VMEM((2, 2, 64, WIDTH), BF16),
            pltpu.VMEM((2, 64, WIDTH // 2), BF16),
            pltpu.VMEM((2, 128, WIDTH), F32),
            pltpu.VMEM((2, 128, WIDTH), BF16),
            pltpu.VMEM((2, 128, WIDTH), BF16),
            dma((q,)),
            dma((3,)),
            dma((2,)), dma((2,)),
            dma((q,)), dma((q,)),
            dma((NZ,)), dma((NZ,)),
            dma((q, NZ)), dma((q, NZ)),
            dma((q, 3, NX)), dma((q, 3, NX)),
            dma((q, 3)), dma((q, 3)),
            dma((q,)), dma((q,)),
            dma((q, 3, NX)), dma((q, 3, NX)),
            dma((q, NZ)), dma((q, NZ)),
        ],
        compiler_params=pltpu.CompilerParams(
            collective_id=0, has_side_effects=True, vmem_limit_bytes=60 * 2**20
        ),
        name="routed_layer",
    )(*args)


def body(tok_a, tok_b, ids_a, ids_b, gates_a, gates_b, gate_proj, up_proj, down_proj):
    small = [jnp.transpose(v, (0, 1, 3, 2)) for v in (ids_a, ids_b, gates_a, gates_b)]
    done = layer(tok_a, tok_b, *small, gate_proj, up_proj, down_proj)
    return pl.pallas_call(
        hand_over,
        out_shape=tuple(jax.ShapeDtypeStruct(v.shape, v.dtype) for v in done),
        name="hand_over",
    )(*done)


def solution(mesh):
    states = P("section", "expert", None)
    routes = P(None, None, "expert", None)
    weights = P("section", "expert", None, None)
    return jax.shard_map(
        body,
        mesh=mesh,
        in_specs=(states, states, routes, routes, routes, routes, weights, weights, weights),
        out_specs=(states, states),
        check_vma=False,
    )
```
